128 devices in a mesh: gx: 16 (over z, x), gy: 8 (over y, core).
Axes of the slice: x: 4, y: 4, z: 4, core: 2. Of those that a mesh axis runs over, the one named last changes fastest.
Arguments:
- atm_fields: float32 [8, 262144], P(None, ('gx', 'gy')), may hold values from -6 to 6
- send_cols: int32 [128, 9, 512], P(('gx', 'gy')), may hold values from 0 to 2047
- pair_count: int32 [128, 9], P(('gx', 'gy')), may hold values from 0 to 512, as said below
- remap_slot: int32 [4, 1024, 1024], P(None, 'gx', 'gy'), may hold values from 0 to 4607, as said below
- remap_weight: float32 [4, 1024, 1024], P(None, 'gx', 'gy'), may hold values from 0.05 to 0.5
- land_mask: int32 [1024, 1024], P('gx', 'gy'), may hold values 0 or 1
- tracers: float32 [2, 32, 1024, 1024], P(None, None, 'gx', 'gy'), may hold values from -6 to 6
- kappa: float32 [32, 1024, 1024], P(None, 'gx', 'gy'), may hold values from 0.02 to 0.2
Outputs:
- atm_flux: float32 [4, 262144], P(None, ('gx', 'gy'))
- tracers_out: float32 [2, 32, 1024, 1024], P(None, None, 'gx', 'gy')
The draws below stay inside these ranges and needn't reach their ends.
Inputs may be any that keep to these rules, and one draw needn't show every extreme that they name: pair_count[s, o] is 0 exactly where offset o leads from device s out of the device grid; inside it, it is 512 for offsets 4 and 8 and between 128 and 512 for the others. So a device sends to and receives from its own position and its eight neighbours in the device grid only. `remap_slot`: every intersection names an offset o whose source device lies inside the device grid and a slot j below pair_count of that source and offset.
All inputs are finite; a program needn't handle non-finite values. No bound on the sum of `land_mask` on one device may be relied on, other than what follows from the above.
Results may differ from the reference program's by a relative error of at most 0.00002.
Values sent between devices are 32-bit elements; how exact they have to be, the bound alone decides.
A program may use at most 128 MiB of HBM per device.

```python
import math
import jax
import jax.numpy as jnp
from jax import lax

AC = 2048
SLOT = 512
NF = 8
NFLUX = 4
K = 4
CX = 64
CY = 128
LEV = 32
STEPS = 4
DEV_ALL = 128
ATOT = 262144
NX = 1024
NY = 1024
N_GX = 16
N_GY = 8


def pair_table(key):
    source = jnp.arange(DEV_ALL, dtype=jnp.int32)[:, None]
    offset = jnp.arange(9, dtype=jnp.int32)[None, :]
    target_x = source // N_GY + offset // 3 - 1
    target_y = source % N_GY + offset % 3 - 1
    inside = (target_x >= 0) & (target_x < N_GX) & (target_y >= 0) & (target_y < N_GY)
    base = jax.random.randint(jax.random.fold_in(key, 21), (DEV_ALL, 9), SLOT // 4, SLOT + 1)
    full = (offset == 4) | (offset == 8)
    counts = jnp.where(full, SLOT, base)
    return jnp.where(inside, counts, 0).astype(jnp.int32)


def draw_pair_count(key, part):
    return pair_table(key)


def draw_remap_slot(key, part):
    counts = pair_table(key)
    block_x = (jnp.arange(NX, dtype=jnp.int32) // CX)[None, :, None]
    block_y = (jnp.arange(NY, dtype=jnp.int32) // CY)[None, None, :]
    off_x = jax.random.randint(jax.random.fold_in(key, 22), (K, NX, NY), -1, 2)
    off_y = jax.random.randint(jax.random.fold_in(key, 23), (K, NX, NY), -1, 2)
    good_x = (block_x - off_x >= 0) & (block_x - off_x < N_GX)
    good_y = (block_y - off_y >= 0) & (block_y - off_y < N_GY)
    off_x = jnp.where(good_x, off_x, 0)
    off_y = jnp.where(good_y, off_y, 0)
    offset = (off_x + 1) * 3 + (off_y + 1)
    source = (block_x - off_x) * N_GY + (block_y - off_y)
    count = counts[source, offset]
    raw = jax.random.randint(jax.random.fold_in(key, 24), (K, NX, NY), 0, 1 << 20)
    within = raw % count
    return (offset * SLOT + within).astype(jnp.int32)


def touch_ends(values, own_key, least, top_value):
    longest = values.shape.index(max(values.shape))
    spots = []
    for shift in (0, 1):
        where = [jax.random.randint(jax.random.fold_in(own_key, axis), (), 0, length) for axis, length in enumerate(values.shape)]
        where[longest] = (where[longest] + shift) % values.shape[longest]
        spots.append(tuple(where))
    return values.at[spots[0]].set(least).at[spots[1]].set(top_value)


def block_levels(key, shape, pieces, low, high):
    def one(axis_at, blocks):
        steps = jax.random.uniform(jax.random.fold_in(jax.random.fold_in(key, 6), axis_at), (blocks,), jnp.float32, low / len(pieces), high / len(pieces))
        return jnp.repeat(jnp.exp(steps), shape[axis_at] // blocks).reshape((-1,) + (1,) * (len(shape) - axis_at - 1))

    level = one(*pieces[0])
    for cut in pieces[1:]:
        level = level * one(*cut)
    return level


def gaussian(rng, extent, width, most, cuts=(), held_as=jnp.bfloat16):
    entries = jax.random.normal(rng, extent, jnp.float32) * width
    if len(cuts) > 0:
        entries = block_levels(rng, extent, cuts, -0.22, 0.18) * entries
    return jnp.clip(entries, min=-most, max=most).astype(held_as)


def setup_inputs(seed: int = 0) -> dict:
    splits = jax.random.split(jax.random.key(seed), 9)
    return {
        "atm_fields": gaussian(splits[0], (NF, ATOT), 1.0, 6.0, ((1, 128),), jnp.float32),
        "send_cols": touch_ends(jax.random.randint(splits[1], (DEV_ALL, 9, SLOT), 0, AC), jax.random.fold_in(splits[1], 1), 0, AC - 1).astype(jnp.int32),
        "pair_count": draw_pair_count(jax.random.fold_in(splits[8], 71), 0),
        "remap_slot": draw_remap_slot(jax.random.fold_in(splits[8], 71), 0),
        "remap_weight": jnp.clip(jnp.exp(math.log(0.5) - 2.3025851 * jax.random.uniform(splits[4], (K, NX, NY), jnp.float32) ** block_levels(splits[4], (K, NX, NY), ((1, 16), (2, 8)), -0.2, 0.2)), 0.05, 0.5),
        "land_mask": touch_ends((jax.random.randint(splits[5], (NX, NY), 0, 10) < 7).astype(jnp.int32), jax.random.fold_in(splits[5], 1), 0, 1),
        "tracers": gaussian(splits[6], (2, LEV, NX, NY), 1.0, 6.0, ((2, 16), (3, 8)), jnp.float32),
        "kappa": jnp.clip(jnp.exp(math.log(0.2) - 2.3025851 * jax.random.uniform(splits[7], (LEV, NX, NY), jnp.float32) ** block_levels(splits[7], (LEV, NX, NY), ((1, 16), (2, 8)), -0.2, 0.2)), 0.02, 0.2),
    }


vertical_mix = 0.05
force_rate = 0.05

def interface_transfer_rate(quantity_grids, topmost_warmth, topmost_saltiness, ocean_cell_indicator):
    breeze_speed = jnp.sqrt(quantity_grids[0] * quantity_grids[0] + quantity_grids[1] * quantity_grids[1] + 1.0)
    thermal_energy_gain = breeze_speed * (quantity_grids[2] - topmost_warmth) + quantity_grids[4] + quantity_grids[5]
    water = breeze_speed * (quantity_grids[3] - 0.2 * topmost_saltiness) - quantity_grids[6]
    stress_x = breeze_speed * quantity_grids[0] + 0.5 * quantity_grids[7]
    stress_y = breeze_speed * quantity_grids[1] - 0.5 * quantity_grids[7]
    return jnp.stack([thermal_energy_gain, water, stress_x, stress_y]) * ocean_cell_indicator

def update(cpad, kpad, ocean_cell_indicator, forcing):
    center = cpad[:, :, 1:-1, 1:-1]
    kc = kpad[:, 1:-1, 1:-1]
    lap = jnp.sqrt(kc * kpad[:, 2:, 1:-1]) * (cpad[:, :, 2:, 1:-1] - center)
    lap = lap + jnp.sqrt(kc * kpad[:, :-2, 1:-1]) * (cpad[:, :, :-2, 1:-1] - center)
    lap = lap + jnp.sqrt(kc * kpad[:, 1:-1, 2:]) * (cpad[:, :, 1:-1, 2:] - center)
    lap = lap + jnp.sqrt(kc * kpad[:, 1:-1, :-2]) * (cpad[:, :, 1:-1, :-2] - center)
    above = jnp.concatenate([center[:, :1], center[:, :-1]], 1)
    below = jnp.concatenate([center[:, 1:], center[:, -1:]], 1)
    fresh = center + lap + vertical_mix * (above + below - 2.0 * center) * ocean_cell_indicator
    return jnp.concatenate([fresh[:, :1] + forcing[:, None], fresh[:, 1:]], 1)

def reference(atm_fields, send_cols, pair_count, remap_slot, remap_weight, land_mask, tracers, kappa):
    ndev = N_GX * N_GY
    slot_iota = lax.broadcasted_iota(jnp.int32, (ndev, 9, SLOT), 2)
    live = (slot_iota < pair_count[:, :, None]).astype(jnp.float32)
    source = lax.broadcasted_iota(jnp.int32, (ndev, 9, SLOT), 0)
    global_col = (source * AC + send_cols).astype(jnp.int32)
    packed = atm_fields[:, global_col] * live
    packed = packed.reshape(NF, ndev * 9 * SLOT)
    xpos = lax.broadcasted_iota(jnp.int32, (NX, NY), 0) // CX
    ypos = lax.broadcasted_iota(jnp.int32, (NX, NY), 1) // CY
    ocean_cell_indicator = land_mask.astype(jnp.float32)
    remapped = jnp.zeros((NF, NX, NY), jnp.float32)
    flat_all = []
    for k in range(K):
        offset = remap_slot[k] // SLOT
        within = remap_slot[k] % SLOT
        off_x = offset // 3 - 1
        off_y = offset % 3 - 1
        src = (xpos - off_x) * N_GY + (ypos - off_y)
        flat = ((src * 9 + offset) * SLOT + within).astype(jnp.int32)
        flat_all.append(flat)
        remapped = remapped + remap_weight[k] * packed[:, flat]
    flux = interface_transfer_rate(remapped, tracers[0, 0], tracers[1, 0], ocean_cell_indicator)
    back = jnp.zeros((NFLUX, ndev * 9 * SLOT), jnp.float32)
    for k in range(K):
        back = back.at[:, flat_all[k]].add(remap_weight[k] * flux)
    back = back.reshape(NFLUX, ndev, 9, SLOT) * live
    atm_flux = jnp.zeros((NFLUX, ATOT), jnp.float32).at[:, global_col].add(back)
    forcing = force_rate * jnp.stack([flux[0], -flux[1]])
    kmask = kappa * ocean_cell_indicator[None]
    kpad = jnp.pad(kmask, ((0, 0), (1, 1), (1, 1)))
    results = []
    for tracer in range(2):
        state = tracers[tracer:tracer + 1]
        for step in range(STEPS):
            cpad = jnp.pad(state, ((0, 0), (0, 0), (1, 1), (1, 1)))
            state = update(cpad, kpad, ocean_cell_indicator, forcing[tracer:tracer + 1])
        results.append(state)
    return (atm_flux, jnp.concatenate(results, 0))
```

```python
import functools

import jax
import jax.numpy as jnp
from jax import lax
from jax.experimental import pallas as pl
from jax.experimental.pallas import tpu as pltpu
from jax.sharding import PartitionSpec as P

MESH = pl.DeviceIdType.MESH
F32, BF16, I32 = jnp.float32, jnp.bfloat16, jnp.int32
NFIELD, AC, SLOT, K, CX, CY, LEV, STEPS = 8, 2048, 512, 4, 64, 128, 32, 4
OFFSETS = [(o // 3 - 1, o % 3 - 1) for o in range(9)]
AROUND = [o for o in range(9) if o != 4]
XT = CX // 8
GROUPS = LEV // 4
PAD = CX + 16


def lanes(shape):
    return lax.broadcasted_iota(I32, shape, len(shape) - 1)


def rows(shape):
    return lax.broadcasted_iota(I32, shape, len(shape) - 2)


def split_pair(v):
    head = v.astype(BF16).astype(F32)
    return jnp.where(rows(v.shape) < 4, head, v - head)


def onehot_rows(index, count):
    return jnp.where(rows((count, 128)) == index, 1.0, 0.0).astype(BF16)


def spread(pair, high, count):
    parts = [jnp.where(high == h, pair, 0.0) for h in range(count)]
    return jnp.concatenate(parts, 0).astype(BF16)


def kernel(
    pc_ref, atm_hbm, cols_hbm, slot_hbm, weight_hbm, land_hbm, tr_hbm, kap_hbm,
    flux_hbm, out_hbm,
    atm, cols, slot, weight, land, tr, kap, aflux,
    psend, precv, bsend, bret, remap, flux8, force,
    s_ref, a_ref, b_ref, c_one, c_two, c_out, u_one, u_two, comb,
    spread_s, onehot_s,
    xsend, xrecv, ysend, yrecv, sxsend, sxrecv, sysend, syrecv,
    in_sem, out_sem, ps_sem, pr_sem, bs_sem, br_sem, hs_sem, hr_sem,
):
    gx, gy = lax.axis_index("gx"), lax.axis_index("gy")
    n_gx, n_gy = lax.axis_size("gx"), lax.axis_size("gy")

    def inside(dx, dy):
        ok = None
        for at, d, n in ((gx, dx, n_gx), (gy, dy, n_gy)):
            c = at > 0 if d < 0 else at < n - 1 if d > 0 else None
            if c is not None:
                ok = c if ok is None else ok & c
        return ok

    sources = (atm_hbm, cols_hbm, slot_hbm, weight_hbm, land_hbm, tr_hbm, kap_hbm)
    targets = (atm, cols, slot, weight, land, tr, kap)
    loads = [pltpu.make_async_copy(a, b, in_sem.at[i]) for i, (a, b) in enumerate(zip(sources, targets))]
    for i in (0, 1, 4, 6, 5, 2, 3):
        loads[i].start()

    barrier = pltpu.get_barrier_semaphore()
    for o in AROUND:
        dx, dy = OFFSETS[o]

        @pl.when(inside(dx, dy))
        def _():
            pl.semaphore_signal(barrier, inc=1, device_id=(gx + dx, gy + dy), device_id_type=MESH)

    for side, missing in ((0, gx == 0), (1, gx == n_gx - 1)):
        @pl.when(missing)
        def _():
            for step in range(STEPS):
                xrecv[step, side] = jnp.zeros((2 * LEV, CY), F32)
            sxrecv[side] = jnp.zeros((LEV, CY), F32)
    for side, missing in ((0, gy == 0), (1, gy == n_gy - 1)):
        @pl.when(missing)
        def _():
            for step in range(STEPS):
                yrecv[step, side] = jnp.zeros((GROUPS, 8, 128), F32)
            syrecv[side] = jnp.zeros((LEV // 8, 8, 128), F32)

    def live(o, base, width):
        count = jnp.broadcast_to(pc_ref[0:1, o:o + 1], (8, width))
        return lanes((8, width)) + base < count

    loads[0].wait()
    loads[1].wait()
    for o in range(9):
        for q in range(SLOT // 128):
            index = jnp.broadcast_to(cols[0, o:o + 1, q * 128:q * 128 + 128], (8, 128))
            low, high = index & 127, index >> 7
            r = jnp.zeros((8, 128), F32)
            for h in range(AC // 128):
                got = jnp.take_along_axis(atm[:, h * 128:h * 128 + 128], low, axis=1, mode="promise_in_bounds")
                r = jnp.where(high == h, got, r)
            r = jnp.where(live(o, q * 128, 128), r, 0.0)
            if o == 4:
                precv[o, :, q * 128:q * 128 + 128] = r
            else:
                psend[o, :, q * 128:q * 128 + 128] = r

    loads[4].wait()
    loads[6].wait()
    loads[5].wait()
    lane = lanes((8, 128))

    def edge(acc, v, i):
        turned = pltpu.roll(v, 2 * i + 1, 1)
        return jnp.where((lane == 2 * i) | (lane == 2 * i + 1), turned, acc)

    def start_s(g, c):
        acc = jnp.zeros((8, 128), F32)
        for dl in range(8):
            lev = g * 8 + dl
            for xt in range(XT):
                at = slice(xt * 8, xt * 8 + 8)
                wet = land[at, :].astype(F32)
                v = jnp.sqrt(kap[lev, at, :] * wet)
                s_ref[pl.ds(pl.multiple_of(lev * PAD + 8 + xt * 8, 8), 8), :] = v
                acc = edge(acc, v, dl * 8 + xt)
        sysend[g] = acc
        return c

    lax.fori_loop(0, LEV // 8, start_s, 0)

    def start_u(g, c):
        acc = jnp.zeros((8, 128), F32)
        for dl in range(4):
            lev = g * 4 + dl
            for xt in range(XT):
                s = s_ref[pl.ds(pl.multiple_of(lev * PAD + 8 + xt * 8, 8), 8), :]
                for t in range(2):
                    u = s * tr[t, lev, xt * 8:xt * 8 + 8, :]
                    u_one[pl.ds(pl.multiple_of((t * LEV + lev) * PAD + 8 + xt * 8, 8), 8), :] = u
                    acc = edge(acc, u, dl * 16 + t * 8 + xt)
        ysend[0, g] = acc
        return c

    lax.fori_loop(0, GROUPS, start_u, 0)

    for xt in range(XT):
        at = slice(xt * 8, xt * 8 + 8)
        b_ref[at, :] = 0.05 * land[at, :].astype(F32)

    def edge_rows(src, dst, levels):
        for j in range(levels // 8):
            dst[0, j * 8:j * 8 + 8, :] = src[pl.ds(j * 8 * PAD + 8 + CX - 1, 8, stride=PAD), :]
            dst[1, j * 8:j * 8 + 8, :] = src[pl.ds(j * 8 * PAD + 8, 8, stride=PAD), :]

    def halo_rows(src, dst, levels):
        for j in range(levels // 8):
            dst[pl.ds(j * 8 * PAD + 7, 8, stride=PAD), :] = src[0, j * 8:j * 8 + 8, :]
            dst[pl.ds(j * 8 * PAD + 8 + CX, 8, stride=PAD), :] = src[1, j * 8:j * 8 + 8, :]

    def halo_copies(xs, xr, ys, yr, n):
        made = []
        for side, (dx, dy) in enumerate(((1, 0), (-1, 0), (0, 1), (0, -1))):
            src = xs.at[side] if side < 2 else ys
            dst = xr.at[side] if side < 2 else yr.at[side - 2]
            copy = pltpu.make_async_remote_copy(
                src_ref=src, dst_ref=dst, send_sem=hs_sem.at[n, side], recv_sem=hr_sem.at[n, side],
                device_id=(gx + dx, gy + dy), device_id_type=MESH)
            made.append((inside(dx, dy), inside(-dx, -dy), copy))
        return made

    def offset_copies(src, dst, ss, rs, sign):
        made = []
        for o in AROUND:
            dx, dy = OFFSETS[o][0] * sign, OFFSETS[o][1] * sign
            copy = pltpu.make_async_remote_copy(
                src_ref=src.at[o], dst_ref=dst.at[o], send_sem=ss.at[o], recv_sem=rs.at[o],
                device_id=(gx + dx, gy + dy), device_id_type=MESH)
            made.append((inside(dx, dy), inside(-dx, -dy), copy))
        return made

    def start(copies):
        for can, _, copy in copies:
            pl.when(can)(copy.start)

    def received(copies):
        for _, comes, copy in copies:
            pl.when(comes)(copy.wait_recv)

    def sent(copies):
        for can, _, copy in copies:
            pl.when(can)(copy.wait_send)

    wide = 1 + (gx > 0).astype(I32) + (gx < n_gx - 1).astype(I32)
    high = 1 + (gy > 0).astype(I32) + (gy < n_gy - 1).astype(I32)
    pl.semaphore_wait(barrier, wide * high - 1)

    packs = offset_copies(psend, precv, ps_sem, pr_sem, 1)
    start(packs)
    edge_rows(s_ref, sxsend, LEV)
    s_halos = halo_copies(sxsend, sxrecv, sysend, syrecv, STEPS)
    start(s_halos)
    edge_rows(u_one, xsend.at[0], 2 * LEV)
    u_halos = [halo_copies(xsend.at[n], xrecv.at[n], ysend.at[n], yrecv.at[n], n) for n in range(STEPS)]
    start(u_halos[0])

    def columns_in(src, groups):
        for g in range(groups):
            comb[g] = jnp.where(lane % 2 == 1, pltpu.roll(src[0, g], 1, 1), pltpu.roll(src[1, g], 127, 1))

    def across(u, packed, i):
        halo = pltpu.roll(packed, 127 - 2 * i, 1)
        left = jnp.where(lane == 0, halo, pltpu.roll(u, 1, 1))
        right = jnp.where(lane == 127, halo, pltpu.roll(u, 127, 1))
        return left + right

    received(s_halos)
    halo_rows(sxrecv, s_ref, LEV)
    columns_in(syrecv, LEV // 8)

    def centre(g, c):
        packed = comb[g]
        for dl in range(8):
            lev = g * 8 + dl
            for xt in range(XT):
                base = lev * PAD + 8 + xt * 8
                s = s_ref[pl.ds(pl.multiple_of(base, 8), 8), :]
                total = across(s, packed, dl * 8 + xt) + s_ref[pl.ds(base - 1, 8), :] + s_ref[pl.ds(base + 1, 8), :]
                a_ref[lev, xt * 8:xt * 8 + 8, :] = 1.0 - s * total - 2.0 * b_ref[xt * 8:xt * 8 + 8, :]
        return c

    lax.fori_loop(0, LEV // 8, centre, 0)

    loads[2].wait()
    loads[3].wait()
    received(packs)

    def gather(i, c):
        for xx in range(4):
            x = i * 4 + xx
            acc = jnp.zeros((8, 128), F32)
            for k in range(K):
                index = jnp.broadcast_to(slot[k, pl.ds(x, 1), :], (8, 128))
                low, high = index & 127, index >> 7
                r = jnp.zeros((8, 128), F32)
                for h in range(36):
                    table = precv[h // 4, :, (h % 4) * 128:(h % 4) * 128 + 128]
                    got = jnp.take_along_axis(table, low, axis=1, mode="promise_in_bounds")
                    r = jnp.where(high == h, got, r)
                acc = acc + jnp.broadcast_to(weight[k, pl.ds(x, 1), :], (8, 128)) * r
            remap[pl.ds(pl.multiple_of(x * 8, 8), 8), :] = acc
        return c

    lax.fori_loop(0, CX // 4, gather, 0)

    for xt in range(XT):
        at = slice(xt * 8, xt * 8 + 8)
        r = [remap[pl.ds(xt * 64 + f, 8, stride=8), :] for f in range(NFIELD)]
        wet = land[at, :].astype(F32)
        ws = jnp.sqrt(r[0] * r[0] + r[1] * r[1] + 1.0)
        heat = (ws * (r[2] - tr[0, 0, at, :]) + r[4] + r[5]) * wet
        water = (ws * (r[3] - 0.2 * tr[1, 0, at, :]) - r[6]) * wet
        sx = (ws * r[0] + 0.5 * r[7]) * wet
        sy = (ws * r[1] - 0.5 * r[7]) * wet
        for g, v in enumerate((heat, water, sx, sy)):
            flux8[pl.ds(xt * 64 + g, 8, stride=8), :] = v
            flux8[pl.ds(xt * 64 + g + 4, 8, stride=8), :] = v
        force[0, 0, at, :] = 0.05 * heat
        force[0, 1, at, :] = -0.05 * water
        force[1, 0, at, :] = jnp.zeros((8, CY), F32)
        force[1, 1, at, :] = jnp.zeros((8, CY), F32)

    def diffuse(step, c_src, c_dst, u_src, u_dst):
        received(u_halos[step])
        halo_rows(xrecv.at[step], u_src, 2 * LEV)
        columns_in(yrecv.at[step], GROUPS)
        last = step == STEPS - 1

        def group(g, c):
            packed = comb[g]
            acc = jnp.zeros((8, 128), F32)
            added = jnp.minimum(g, 1)
            for dl in range(4):
                lev = g * 4 + dl
                above, below = jnp.maximum(lev - 1, 0), jnp.minimum(lev + 1, LEV - 1)
                for xt in range(XT):
                    at = slice(xt * 8, xt * 8 + 8)
                    s = s_ref[pl.ds(pl.multiple_of(lev * PAD + 8 + xt * 8, 8), 8), :]
                    a, b = a_ref[lev, at, :], b_ref[at, :]
                    for t in range(2):
                        base = (t * LEV + lev) * PAD + 8 + xt * 8
                        i = dl * 16 + t * 8 + xt
                        u = u_src[pl.ds(pl.multiple_of(base, 8), 8), :]
                        total = across(u, packed, i) + u_src[pl.ds(base - 1, 8), :] + u_src[pl.ds(base + 1, 8), :]
                        new = a * c_src[t, lev, at, :] + s * total + b * (c_src[t, above, at, :] + c_src[t, below, at, :])
                        if dl == 0:
                            new = new + force[added, t, at, :]
                        c_dst[t, lev, at, :] = new
                        if not last:
                            u = s * new
                            u_dst[pl.ds(pl.multiple_of(base, 8), 8), :] = u
                            acc = edge(acc, u, i)
            if not last:
                ysend[step + 1, g] = acc
            return c

        lax.fori_loop(0, GROUPS, group, 0)
        if not last:
            edge_rows(u_dst, xsend.at[step + 1], 2 * LEV)
            start(u_halos[step + 1])

    diffuse(0, tr, c_one, u_one, u_two)

    def scatter_rows(i, c):
        for xx in range(8):
            x = i * 8 + xx
            for k in range(K):
                index = slot[k, pl.ds(x, 1), :]
                v = jnp.broadcast_to(weight[k, pl.ds(x, 1), :], (8, 128)) * flux8[pl.ds(pl.multiple_of(x * 8, 8), 8), :]
                to = slice((xx * K + k) * 128, (xx * K + k) * 128 + 128)
                onehot_s[:, to] = onehot_rows(index & 255, 256)
                spread_s[:, to] = spread(split_pair(v), jnp.broadcast_to(index >> 8, (8, 128)), 18)
        return c + lax.dot_general(
            spread_s[:, :4096], onehot_s[:, :4096], (((1,), (1,)), ((), ())), preferred_element_type=F32)

    back = lax.fori_loop(0, CX // 8, scatter_rows, jnp.zeros((144, 256), F32))
    for o in range(9):
        for half in range(2):
            h = o * 2 + half
            v = back[h * 8:h * 8 + 4] + back[h * 8 + 4:h * 8 + 8]
            if o == 4:
                bret[o, half * 4:half * 4 + 4, :] = v
            else:
                bsend[o, half * 4:half * 4 + 4, :] = v
    backs = offset_copies(bsend, bret, bs_sem, br_sem, -1)
    start(backs)

    diffuse(1, c_one, c_two, u_two, u_one)

    received(backs)
    for o in range(9):
        for q in range(4):
            half, at = q // 2, slice((q % 2) * 128, (q % 2) * 128 + 128)
            v = bret[o, :, at]
            swapped = pltpu.roll(v, 4, 0)
            first = rows((8, 128)) < 4
            v = jnp.where(first, v, swapped) if half == 0 else jnp.where(first, swapped, v)
            v = jnp.where(live(o, q * 128, 128), v, 0.0)
            index = cols[0, o:o + 1, q * 128:q * 128 + 128]
            to = slice((o * 4 + q) * 128, (o * 4 + q) * 128 + 128)
            onehot_s[:, to] = onehot_rows(index & 255, 256)
            spread_s[:64, to] = spread(split_pair(v), jnp.broadcast_to(index >> 8, (8, 128)), 8)
    cells = 36 * 128
    ends = lax.dot_general(
        spread_s[:64, :cells], onehot_s[:, :cells], (((1,), (1,)), ((), ())), preferred_element_type=F32)
    for h in range(8):
        aflux[:, h * 256:h * 256 + 256] = ends[h * 8:h * 8 + 4] + ends[h * 8 + 4:h * 8 + 8]
    flux_out = pltpu.make_async_copy(aflux, flux_hbm, out_sem.at[0])
    flux_out.start()

    diffuse(2, c_two, c_one, u_one, u_two)
    diffuse(3, c_one, c_out, u_two, u_one)
    state_out = pltpu.make_async_copy(c_out, out_hbm, out_sem.at[1])
    state_out.start()
    sent(packs)
    sent(s_halos)
    sent(backs)
    for copies in u_halos:
        sent(copies)
    flux_out.wait()
    state_out.wait()


def per_device(atm_fields, send_cols, pair_count, remap_slot, remap_weight, land_mask, tracers, kappa):
    V, S = pltpu.VMEM, pltpu.SemaphoreType
    hbm = pl.BlockSpec(memory_space=pl.ANY)
    return pl.pallas_call(
        kernel,
        out_shape=(
            jax.ShapeDtypeStruct((4, AC), F32),
            jax.ShapeDtypeStruct((2, LEV, CX, CY), F32),
        ),
        in_specs=[pl.BlockSpec(memory_space=pltpu.VMEM)] + [hbm] * 7,
        out_specs=(hbm, hbm),
        scratch_shapes=[
            V((8, AC), F32), V((1, 9, SLOT), I32), V((K, CX, CY), I32), V((K, CX, CY), F32), V((CX, CY), I32),
            V((2, LEV, CX, CY), F32), V((LEV, CX, CY), F32), V((4, AC), F32),
            V((9, 8, SLOT), F32), V((9, 8, SLOT), F32), V((9, 8, 256), F32), V((9, 8, 256), F32),
            V((CX * 8, CY), F32), V((CX * 8, CY), F32), V((2, 2, CX, CY), F32),
            V((LEV * PAD, CY), F32), V((LEV, CX, CY), F32), V((CX, CY), F32),
            V((2, LEV, CX, CY), F32), V((2, LEV, CX, CY), F32), V((2, LEV, CX, CY), F32),
            V((2 * LEV * PAD, CY), F32), V((2 * LEV * PAD, CY), F32), V((GROUPS, 8, 128), F32),
            V((144, 36 * 128), BF16), V((256, 36 * 128), BF16),
            V((STEPS, 2, 2 * LEV, CY), F32), V((STEPS, 2, 2 * LEV, CY), F32),
            V((STEPS, GROUPS, 8, 128), F32), V((STEPS, 2, GROUPS, 8, 128), F32),
            V((2, LEV, CY), F32), V((2, LEV, CY), F32), V((LEV // 8, 8, 128), F32), V((2, LEV // 8, 8, 128), F32),
            S.DMA((7,)), S.DMA((2,)), S.DMA((9,)), S.DMA((9,)), S.DMA((9,)), S.DMA((9,)),
            S.DMA((STEPS + 1, 4)), S.DMA((STEPS + 1, 4)),
        ],
        compiler_params=pltpu.CompilerParams(
            collective_id=0, has_side_effects=True, vmem_limit_bytes=56 << 20),
        name="couple",
    )(pair_count, atm_fields, send_cols, remap_slot, remap_weight, land_mask, tracers, kappa)


def solution(mesh):
    return jax.shard_map(
        per_device,
        mesh=mesh,
        in_specs=(
            P(None, ("gx", "gy")),
            P(("gx", "gy"), None, None),
            P(("gx", "gy"), None),
            P(None, "gx", "gy"),
            P(None, "gx", "gy"),
            P("gx", "gy"),
            P(None, None, "gx", "gy"),
            P(None, "gx", "gy"),
        ),
        out_specs=(P(None, ("gx", "gy")), P(None, None, "gx", "gy")),
        check_vma=False,
    )
```

```python
import functools

import jax
import jax.numpy as jnp
from jax import lax
from jax.experimental import pallas as pl
from jax.experimental.pallas import tpu as pltpu
from jax.sharding import PartitionSpec as P

MESH = pl.DeviceIdType.MESH
F32, BF16, I32 = jnp.float32, jnp.bfloat16, jnp.int32
NFIELD, AC, SLOT, K, CX, CY, LEV, STEPS = 8, 2048, 512, 4, 64, 128, 32, 4
OFFSETS = [(o // 3 - 1, o % 3 - 1) for o in range(9)]
AROUND = [o for o in range(9) if o != 4]
XT = CX // 8
GROUPS = LEV // 4
GX, SX = 16, 16
PAD = CX + 16


def lanes(shape):
    return lax.broadcasted_iota(I32, shape, len(shape) - 1)


def rows(shape):
    return lax.broadcasted_iota(I32, shape, len(shape) - 2)


def split_pair(v):
    head = v.astype(BF16).astype(F32)
    return jnp.where(rows(v.shape) < 4, head, v - head)


def onehot_rows(index, count):
    at = rows((count, 128)).astype(F32).astype(BF16)
    low = jnp.broadcast_to(index.astype(F32), (16, 128)).astype(BF16)
    low = jnp.concatenate([low] * (count // 16), 0)
    return jnp.where(at == low, jnp.ones((), BF16), jnp.zeros((), BF16))


def spread(pair, high, count):
    two = jnp.concatenate([pair, pair], 0).astype(BF16)
    at = (jnp.broadcast_to(high, (16, 128)) - rows((16, 128)) // 8).astype(F32).astype(BF16)
    zero = jnp.zeros((), BF16)
    return jnp.concatenate([jnp.where(at == jnp.asarray(2 * q, BF16), two, zero) for q in range(count // 2)], 0)


def kernel(
    pc_ref, atm_hbm, cols_hbm, slot_hbm, weight_hbm, land_hbm, tr_hbm, kap_hbm,
    aflux, c_out,
    atm, cols, slot, weight, land, tr, kap,
    psend, precv, bsend, bret, remap, flux8, force,
    s_ref, a_ref, b_ref, c_one, c_two, u_one, u_two, comb,
    spread_s, onehot_s, table_s,
    xsend, xrecv, ysend, yrecv, sxsend, sxrecv, sysend, syrecv,
    in_sem, ps_sem, pr_sem, bs_sem, br_sem, hs_sem, hr_sem,
):
    gx, gy = lax.axis_index("gx"), lax.axis_index("gy")
    n_gx, n_gy = lax.axis_size("gx"), lax.axis_size("gy")

    def inside(dx, dy):
        ok = None
        for at, d, n in ((gx, dx, n_gx), (gy, dy, n_gy)):
            c = at > 0 if d < 0 else at < n - 1 if d > 0 else None
            if c is not None:
                ok = c if ok is None else ok & c
        return ok

    sources = (atm_hbm, cols_hbm, slot_hbm, weight_hbm, land_hbm, tr_hbm, kap_hbm)
    targets = (atm, cols, slot, weight, land, tr, kap)
    loads = [pltpu.make_async_copy(a, b, in_sem.at[i]) for i, (a, b) in enumerate(zip(sources, targets))]
    for i in (0, 1, 4, 6, 5, 2, 3):
        loads[i].start()

    barrier = pltpu.get_barrier_semaphore()
    for o in AROUND:
        dx, dy = OFFSETS[o]

        @pl.when(inside(dx, dy))
        def _():
            pl.semaphore_signal(barrier, inc=1, device_id=(gx + dx, gy + dy), device_id_type=MESH)

    for side, missing in ((0, gx == 0), (1, gx == n_gx - 1)):
        @pl.when(missing)
        def _():
            for step in range(STEPS):
                xrecv[step, side] = jnp.zeros((2 * LEV, CY), F32)
            sxrecv[side] = jnp.zeros((LEV, CY), F32)
    for side, missing in ((0, gy == 0), (1, gy == n_gy - 1)):
        @pl.when(missing)
        def _():
            for step in range(STEPS):
                yrecv[step, side] = jnp.zeros((GROUPS, 8, 128), F32)
            syrecv[side] = jnp.zeros((LEV // 8, 8, 128), F32)

    def live(o, base, width):
        count = jnp.broadcast_to(pc_ref[0:1, o:o + 1], (8, width))
        return lanes((8, width)) + base < count

    loads[0].wait()
    loads[1].wait()
    for o in range(9):
        for q in range(SLOT // 128):
            index = jnp.broadcast_to(cols[o, :, q * 128:q * 128 + 128], (8, 128))
            low, high = index & 127, index >> 7
            r = jnp.zeros((8, 128), F32)
            for h in range(AC // 128):
                got = jnp.take_along_axis(atm[:, h * 128:h * 128 + 128], low, axis=1, mode="promise_in_bounds")
                r = jnp.where(high == h, got, r)
            r = jnp.where(live(o, q * 128, 128), r, 0.0)
            if o == 4:
                precv[o, :, q * 128:q * 128 + 128] = r
            else:
                psend[o, :, q * 128:q * 128 + 128] = r

    loads[4].wait()
    loads[6].wait()
    loads[5].wait()
    lane = lanes((8, 128))

    def edge(acc, v, i):
        turned = pltpu.roll(v, 2 * i + 1, 1)
        return jnp.where((lane == 2 * i) | (lane == 2 * i + 1), turned, acc)

    def start_s(g, c):
        acc = jnp.zeros((8, 128), F32)
        for dl in range(8):
            lev = g * 8 + dl
            for xt in range(XT):
                at = slice(xt * 8, xt * 8 + 8)
                wet = land[at, :].astype(F32)
                v = jnp.sqrt(kap[lev, at, :] * wet)
                s_ref[pl.ds(pl.multiple_of(lev * PAD + 8 + xt * 8, 8), 8), :] = v
                acc = edge(acc, v, dl * 8 + xt)
        sysend[g] = acc
        return c

    lax.fori_loop(0, LEV // 8, start_s, 0)

    def edge_columns(src, dst, g, c):
        acc = jnp.zeros((8, 128), F32)
        for dl in range(4):
            lev = g * 4 + dl
            for t in range(2):
                for xt in range(XT):
                    base = (t * LEV + lev) * PAD + 8 + xt * 8
                    acc = edge(acc, src[pl.ds(pl.multiple_of(base, 8), 8), :], dl * 16 + t * 8 + xt)
        dst[g] = acc
        return c

    def start_u(g, c):
        acc = jnp.zeros((8, 128), F32)
        for dl in range(4):
            lev = g * 4 + dl
            for xt in range(XT):
                s = s_ref[pl.ds(pl.multiple_of(lev * PAD + 8 + xt * 8, 8), 8), :]
                for t in range(2):
                    u = s * tr[t, lev, xt * 8:xt * 8 + 8, :]
                    u_one[pl.ds(pl.multiple_of((t * LEV + lev) * PAD + 8 + xt * 8, 8), 8), :] = u
                    acc = edge(acc, u, dl * 16 + t * 8 + xt)
        ysend[0, g] = acc
        return c

    lax.fori_loop(0, GROUPS, start_u, 0)

    for xt in range(XT):
        at = slice(xt * 8, xt * 8 + 8)
        b_ref[at, :] = 0.05 * land[at, :].astype(F32)

    def edge_rows(src, dst, levels):
        for j in range(levels // 8):
            dst[0, j * 8:j * 8 + 8, :] = src[pl.ds(j * 8 * PAD + 8 + CX - 1, 8, stride=PAD), :]
            dst[1, j * 8:j * 8 + 8, :] = src[pl.ds(j * 8 * PAD + 8, 8, stride=PAD), :]

    def halo_rows(src, dst, levels):
        for j in range(levels // 8):
            dst[pl.ds(j * 8 * PAD + 7, 8, stride=PAD), :] = src[0, j * 8:j * 8 + 8, :]
            dst[pl.ds(j * 8 * PAD + 8 + CX, 8, stride=PAD), :] = src[1, j * 8:j * 8 + 8, :]

    def halo_copies(xs, xr, ys, yr, n):
        made = []
        for side, (dx, dy) in enumerate(((1, 0), (-1, 0), (0, 1), (0, -1))):
            src = xs.at[side] if side < 2 else ys
            dst = xr.at[side] if side < 2 else yr.at[side - 2]
            copy = pltpu.make_async_remote_copy(
                src_ref=src, dst_ref=dst, send_sem=hs_sem.at[n, side], recv_sem=hr_sem.at[n, side],
                device_id=(gx + dx, gy + dy), device_id_type=MESH)
            made.append((inside(dx, dy), inside(-dx, -dy), copy))
        return made

    def offset_copies(src, dst, ss, rs, sign):
        made = []
        for o in AROUND:
            dx, dy = OFFSETS[o][0] * sign, OFFSETS[o][1] * sign
            copy = pltpu.make_async_remote_copy(
                src_ref=src.at[o], dst_ref=dst.at[o], send_sem=ss.at[o], recv_sem=rs.at[o],
                device_id=(gx + dx, gy + dy), device_id_type=MESH)
            made.append((inside(dx, dy), inside(-dx, -dy), copy))
        return made

    def start(copies):
        for can, _, copy in copies:
            pl.when(can)(copy.start)

    def received(copies):
        for _, comes, copy in copies:
            pl.when(comes)(copy.wait_recv)

    def sent(copies):
        for can, _, copy in copies:
            pl.when(can)(copy.wait_send)

    wide = 1 + (gx > 0).astype(I32) + (gx < n_gx - 1).astype(I32)
    high = 1 + (gy > 0).astype(I32) + (gy < n_gy - 1).astype(I32)
    pl.semaphore_wait(barrier, wide * high - 1)

    packs = offset_copies(psend, precv, ps_sem, pr_sem, 1)
    start(packs)
    edge_rows(s_ref, sxsend, LEV)
    s_halos = halo_copies(sxsend, sxrecv, sysend, syrecv, STEPS)
    start(s_halos)
    edge_rows(u_one, xsend.at[0], 2 * LEV)
    u_halos = [halo_copies(xsend.at[n], xrecv.at[n], ysend.at[n], yrecv.at[n], n) for n in range(STEPS)]
    start(u_halos[0])

    def columns_in(src, groups):
        for g in range(groups):
            comb[g] = jnp.where(lane % 2 == 1, pltpu.roll(src[0, g], 1, 1), pltpu.roll(src[1, g], 127, 1))

    def across(u, packed, i):
        halo = pltpu.roll(packed, 127 - 2 * i, 1)
        left = jnp.where(lane == 0, halo, pltpu.roll(u, 1, 1))
        right = jnp.where(lane == 127, halo, pltpu.roll(u, 127, 1))
        return left + right

    loads[2].wait()
    loads[3].wait()

    def onehots(i, c):
        for xx in range(4):
            x = i * 4 + xx
            for k in range(K):
                at = pl.ds(pl.multiple_of((x * K + k) * 128, 128), 128)
                onehot_s[:, at] = onehot_rows(slot[k, pl.ds(x, 1), :] & 255, 256)
        return c

    lax.fori_loop(0, CX // 4, onehots, 0)

    received(s_halos)
    halo_rows(sxrecv, s_ref, LEV)
    columns_in(syrecv, LEV // 8)

    def centre(g, c):
        packed = comb[g]
        for dl in range(8):
            lev = g * 8 + dl
            for xt in range(XT):
                base = lev * PAD + 8 + xt * 8
                s = s_ref[pl.ds(pl.multiple_of(base, 8), 8), :]
                total = across(s, packed, dl * 8 + xt) + s_ref[pl.ds(base - 1, 8), :] + s_ref[pl.ds(base + 1, 8), :]
                a_ref[lev, xt * 8:xt * 8 + 8, :] = 1.0 - s * total - 2.0 * b_ref[xt * 8:xt * 8 + 8, :]
        return c

    lax.fori_loop(0, LEV // 8, centre, 0)

    def diffuse(step, c_src, c_dst, u_src, u_dst):
        received(u_halos[step])
        halo_rows(xrecv.at[step], u_src, 2 * LEV)
        columns_in(yrecv.at[step], GROUPS)

        def group(g, c):
            packed = comb[g]
            added = jnp.minimum(g, 1)
            for dl in range(4):
                lev = g * 4 + dl
                above, below = jnp.maximum(lev - 1, 0), jnp.minimum(lev + 1, LEV - 1)
                for xt in range(XT):
                    at = slice(xt * 8, xt * 8 + 8)
                    s = s_ref[pl.ds(pl.multiple_of(lev * PAD + 8 + xt * 8, 8), 8), :]
                    a, b = a_ref[lev, at, :], b_ref[at, :]
                    for t in range(2):
                        base = (t * LEV + lev) * PAD + 8 + xt * 8
                        u = u_src[pl.ds(pl.multiple_of(base, 8), 8), :]
                        total = across(u, packed, dl * 16 + t * 8 + xt) + u_src[pl.ds(base - 1, 8), :] + u_src[pl.ds(base + 1, 8), :]
                        new = a * c_src[t, lev, at, :] + s * total + b * (c_src[t, above, at, :] + c_src[t, below, at, :])
                        if dl == 0 and step > 0:
                            new = new + force[added, t, at, :]
                        c_dst[t, lev, at, :] = new
                        if step < STEPS - 1:
                            u_dst[pl.ds(pl.multiple_of(base, 8), 8), :] = s * new
            return c

        lax.fori_loop(0, GROUPS, group, 0)

    def send_halos(step, src):
        lax.fori_loop(0, GROUPS, functools.partial(edge_columns, src, ysend.at[step]), 0)
        edge_rows(src, xsend.at[step], 2 * LEV)
        start(u_halos[step])

    diffuse(0, tr, c_one, u_one, u_two)

    received(packs)

    table = jnp.concatenate([precv[h // 2, :, (h % 2) * 256:(h % 2) * 256 + 256] for h in range(18)], 0)
    head = table.astype(BF16)
    table_s[0] = head
    table_s[1] = (table - head.astype(F32)).astype(BF16)

    def gather(i, c):
        for xx in range(GX):
            x = i * GX + xx
            hot = onehot_s[:, pl.ds(pl.multiple_of(x * K * 128, 512), K * 128)]
            found = jnp.dot(table_s[0], hot, preferred_element_type=F32) + jnp.dot(table_s[1], hot, preferred_element_type=F32)
            acc = jnp.zeros((8, 128), F32)
            for k in range(K):
                high = jnp.broadcast_to(slot[k, pl.ds(x, 1), :], (8, 128)) >> 8
                r = jnp.zeros((8, 128), F32)
                for h in range(18):
                    r = jnp.where(high == h, found[h * 8:h * 8 + 8, k * 128:k * 128 + 128], r)
                acc = acc + jnp.broadcast_to(weight[k, pl.ds(x, 1), :], (8, 128)) * r
            remap[pl.ds(pl.multiple_of(x * 8, 8), 8), :] = acc
        return c

    lax.fori_loop(0, CX // GX, gather, 0)

    for xt in range(XT):
        at = slice(xt * 8, xt * 8 + 8)
        r = [remap[pl.ds(xt * 64 + f, 8, stride=8), :] for f in range(NFIELD)]
        wet = land[at, :].astype(F32)
        ws = jnp.sqrt(r[0] * r[0] + r[1] * r[1] + 1.0)
        heat = (ws * (r[2] - tr[0, 0, at, :]) + r[4] + r[5]) * wet
        water = (ws * (r[3] - 0.2 * tr[1, 0, at, :]) - r[6]) * wet
        sx = (ws * r[0] + 0.5 * r[7]) * wet
        sy = (ws * r[1] - 0.5 * r[7]) * wet
        for g, v in enumerate((heat, water, sx, sy)):
            flux8[pl.ds(xt * 64 + g, 8, stride=8), :] = v
            flux8[pl.ds(xt * 64 + g + 4, 8, stride=8), :] = v
        for t, v in enumerate((0.05 * heat, -0.05 * water)):
            force[0, t, at, :] = v
            v = c_one[t, 0, at, :] + v
            c_one[t, 0, at, :] = v
            u_two[t * LEV * PAD + 8 + xt * 8:t * LEV * PAD + 16 + xt * 8, :] = s_ref[8 + xt * 8:16 + xt * 8, :] * v
        force[1, 0, at, :] = jnp.zeros((8, CY), F32)
        force[1, 1, at, :] = jnp.zeros((8, CY), F32)

    send_halos(1, u_two)

    def scatter_rows(i, c):
        for xx in range(SX):
            x = i * SX + xx
            for k in range(K):
                v = jnp.broadcast_to(weight[k, pl.ds(x, 1), :], (8, 128)) * flux8[pl.ds(pl.multiple_of(x * 8, 8), 8), :]
                to = slice((xx * K + k) * 128, (xx * K + k) * 128 + 128)
                spread_s[:, to] = spread(split_pair(v), slot[k, pl.ds(x, 1), :] >> 8, 18)
        hot = onehot_s[:, pl.ds(pl.multiple_of(i * (SX * K * 128), 512), SX * K * 128)]
        return c + lax.dot_general(
            spread_s[:, :SX * K * 128], hot, (((1,), (1,)), ((), ())), preferred_element_type=F32)

    back = lax.fori_loop(0, 2, scatter_rows, jnp.zeros((144, 256), F32))
    diffuse(1, c_one, c_two, u_two, u_one)
    send_halos(2, u_one)
    back = scatter_rows(2, back)
    diffuse(2, c_two, c_one, u_one, u_two)
    send_halos(3, u_two)
    back = scatter_rows(3, back)
    for o in range(9):
        for half in range(2):
            h = o * 2 + half
            v = back[h * 8:h * 8 + 4] + back[h * 8 + 4:h * 8 + 8]
            if o == 4:
                bret[o, half * 4:half * 4 + 4, :] = v
            else:
                bsend[o, half * 4:half * 4 + 4, :] = v
    backs = offset_copies(bsend, bret, bs_sem, br_sem, -1)
    start(backs)

    diffuse(3, c_one, c_out, u_two, u_one)

    received(backs)
    for o in range(9):
        for q in range(4):
            half, at = q // 2, slice((q % 2) * 128, (q % 2) * 128 + 128)
            v = bret[o, :, at]
            swapped = pltpu.roll(v, 4, 0)
            first = rows((8, 128)) < 4
            v = jnp.where(first, v, swapped) if half == 0 else jnp.where(first, swapped, v)
            v = jnp.where(live(o, q * 128, 128), v, 0.0)
            index = cols[o, :, q * 128:q * 128 + 128]
            to = slice((o * 4 + q) * 128, (o * 4 + q) * 128 + 128)
            onehot_s[:, to] = onehot_rows(index & 255, 256)
            spread_s[:64, to] = spread(split_pair(v), index >> 8, 8)
    cells = 36 * 128
    ends = lax.dot_general(
        spread_s[:64, :cells], onehot_s[:, :cells], (((1,), (1,)), ((), ())), preferred_element_type=F32)
    for h in range(8):
        aflux[:, h * 256:h * 256 + 256] = ends[h * 8:h * 8 + 4] + ends[h * 8 + 4:h * 8 + 8]

    sent(packs)
    sent(s_halos)
    sent(backs)
    for copies in u_halos:
        sent(copies)


def per_device(atm_fields, send_cols, pair_count, remap_slot, remap_weight, land_mask, tracers, kappa):
    V, S = pltpu.VMEM, pltpu.SemaphoreType
    hbm = pl.BlockSpec(memory_space=pl.ANY)
    return pl.pallas_call(
        kernel,
        out_shape=(
            pltpu.VMEM((4, AC), F32),
            pltpu.VMEM((2, LEV, CX, CY), F32),
        ),
        in_specs=[pl.BlockSpec(memory_space=pltpu.VMEM)] + [hbm] * 7,
        out_specs=(pl.BlockSpec(memory_space=pltpu.VMEM),) * 2,
        scratch_shapes=[
            V((8, AC), F32), V((9, 1, SLOT), I32), V((K, CX, CY), I32), V((K, CX, CY), F32), V((CX, CY), I32),
            V((2, LEV, CX, CY), F32), V((LEV, CX, CY), F32),
            V((9, 8, SLOT), F32), V((9, 8, SLOT), F32), V((9, 8, 256), F32), V((9, 8, 256), F32),
            V((CX * 8, CY), F32), V((CX * 8, CY), F32), V((2, 2, CX, CY), F32),
            V((LEV * PAD, CY), F32), V((LEV, CX, CY), F32), V((CX, CY), F32),
            V((2, LEV, CX, CY), F32), V((2, LEV, CX, CY), F32),
            V((2 * LEV * PAD, CY), F32), V((2 * LEV * PAD, CY), F32), V((GROUPS, 8, 128), F32),
            V((144, 64 * 128), BF16), V((256, CX * K * 128), BF16), V((2, 144, 256), BF16),
            V((STEPS, 2, 2 * LEV, CY), F32), V((STEPS, 2, 2 * LEV, CY), F32),
            V((STEPS, GROUPS, 8, 128), F32), V((STEPS, 2, GROUPS, 8, 128), F32),
            V((2, LEV, CY), F32), V((2, LEV, CY), F32), V((LEV // 8, 8, 128), F32), V((2, LEV // 8, 8, 128), F32),
            S.DMA((7,)), S.DMA((9,)), S.DMA((9,)), S.DMA((9,)), S.DMA((9,)),
            S.DMA((STEPS + 1, 4)), S.DMA((STEPS + 1, 4)),
        ],
        compiler_params=pltpu.CompilerParams(
            collective_id=0, has_side_effects=True, vmem_limit_bytes=52 << 20),
        name="couple",
    )(pair_count, atm_fields, send_cols.transpose(1, 0, 2), remap_slot, remap_weight, land_mask, tracers, kappa)


def solution(mesh):
    return jax.shard_map(
        per_device,
        mesh=mesh,
        in_specs=(
            P(None, ("gx", "gy")),
            P(("gx", "gy"), None, None),
            P(("gx", "gy"), None),
            P(None, "gx", "gy"),
            P(None, "gx", "gy"),
            P("gx", "gy"),
            P(None, None, "gx", "gy"),
            P(None, "gx", "gy"),
        ),
        out_specs=(P(None, ("gx", "gy")), P(None, None, "gx", "gy")),
        check_vma=False,
    )
```

```python
import functools

import jax
import jax.numpy as jnp
from jax import lax
from jax.experimental import pallas as pl
from jax.experimental.pallas import tpu as pltpu
from jax.sharding import PartitionSpec as P

MESH = pl.DeviceIdType.MESH
F32, BF16, I32 = jnp.float32, jnp.bfloat16, jnp.int32
NFIELD, AC, SLOT, K, CX, CY, LEV, STEPS = 8, 2048, 512, 4, 64, 128, 32, 4
OFFSETS = [(o // 3 - 1, o % 3 - 1) for o in range(9)]
AROUND = [o for o in range(9) if o != 4]
XT = CX // 8
GROUPS = LEV // 4
GX, SX = 16, 16
PAD = CX + 16


def lanes(shape):
    return lax.broadcasted_iota(I32, shape, len(shape) - 1)


def rows(shape):
    return lax.broadcasted_iota(I32, shape, len(shape) - 2)


def split_pair(v):
    head = v.astype(BF16).astype(F32)
    return jnp.where(rows(v.shape) < 4, head, v - head)


def onehot_rows(index, count):
    at = rows((count, 128)).astype(F32).astype(BF16)
    low = jnp.broadcast_to(index.astype(F32), (16, 128)).astype(BF16)
    low = jnp.concatenate([low] * (count // 16), 0)
    return jnp.where(at == low, jnp.ones((), BF16), jnp.zeros((), BF16))


def spread(pair, high, count):
    two = jnp.concatenate([pair, pair], 0).astype(BF16)
    at = (jnp.broadcast_to(high, (16, 128)) - rows((16, 128)) // 8).astype(F32).astype(BF16)
    zero = jnp.zeros((), BF16)
    return jnp.concatenate([jnp.where(at == jnp.asarray(2 * q, BF16), two, zero) for q in range(count // 2)], 0)


def kernel(
    pc_ref, atm_hbm, cols_hbm, slot_hbm, weight_hbm, land_hbm, tr_hbm, kap_hbm,
    aflux, c_out,
    atm, cols, slot, weight, land, tr, kap,
    psend, precv, bsend, bret, remap, flux8, force,
    s_ref, a_ref, b_ref, c_one, c_two, u_one, u_two, comb,
    spread_s, onehot_s, table_s, beside_s,
    xsend, xrecv, ysend, yrecv, sxsend, sxrecv, sysend, syrecv,
    in_sem, ps_sem, pr_sem, bs_sem, br_sem, hs_sem, hr_sem,
):
    gx, gy = lax.axis_index("gx"), lax.axis_index("gy")
    n_gx, n_gy = lax.axis_size("gx"), lax.axis_size("gy")

    def inside(dx, dy):
        ok = None
        for at, d, n in ((gx, dx, n_gx), (gy, dy, n_gy)):
            c = at > 0 if d < 0 else at < n - 1 if d > 0 else None
            if c is not None:
                ok = c if ok is None else ok & c
        return ok

    sources = (atm_hbm, cols_hbm, slot_hbm, weight_hbm, land_hbm, tr_hbm, kap_hbm)
    targets = (atm, cols, slot, weight, land, tr, kap)
    loads = [pltpu.make_async_copy(a, b, in_sem.at[i]) for i, (a, b) in enumerate(zip(sources, targets))]
    for i in (0, 1, 4, 6, 5, 2, 3):
        loads[i].start()

    barrier = pltpu.get_barrier_semaphore()
    for o in AROUND:
        dx, dy = OFFSETS[o]

        @pl.when(inside(dx, dy))
        def _():
            pl.semaphore_signal(barrier, inc=1, device_id=(gx + dx, gy + dy), device_id_type=MESH)

    for side, missing in ((0, gx == 0), (1, gx == n_gx - 1)):
        @pl.when(missing)
        def _():
            for step in range(STEPS):
                xrecv[step, side] = jnp.zeros((2 * LEV, CY), F32)
            sxrecv[side] = jnp.zeros((LEV, CY), F32)
    for side, missing in ((0, gy == 0), (1, gy == n_gy - 1)):
        @pl.when(missing)
        def _():
            for step in range(STEPS):
                yrecv[step, side] = jnp.zeros((GROUPS, 8, 128), F32)
            syrecv[side] = jnp.zeros((LEV // 8, 8, 128), F32)

    def live(o, base, width):
        count = jnp.broadcast_to(pc_ref[0:1, o:o + 1], (8, width))
        return lanes((8, width)) + base < count

    loads[0].wait()
    loads[1].wait()
    for o in range(9):
        for q in range(SLOT // 128):
            index = jnp.broadcast_to(cols[o, :, q * 128:q * 128 + 128], (8, 128))
            low, high = index & 127, index >> 7
            r = jnp.zeros((8, 128), F32)
            for h in range(AC // 128):
                got = jnp.take_along_axis(atm[:, h * 128:h * 128 + 128], low, axis=1, mode="promise_in_bounds")
                r = jnp.where(high == h, got, r)
            r = jnp.where(live(o, q * 128, 128), r, 0.0)
            if o == 4:
                precv[o, :, q * 128:q * 128 + 128] = r
            else:
                psend[o, :, q * 128:q * 128 + 128] = r

    loads[4].wait()
    loads[6].wait()
    loads[5].wait()
    lane = lanes((8, 128))

    def edge(acc, v, i):
        turned = pltpu.roll(v, 2 * i + 1, 1)
        return jnp.where((lane == 2 * i) | (lane == 2 * i + 1), turned, acc)

    def start_s(g, c):
        acc = jnp.zeros((8, 128), F32)
        for dl in range(8):
            lev = g * 8 + dl
            for xt in range(XT):
                at = slice(xt * 8, xt * 8 + 8)
                wet = land[at, :].astype(F32)
                v = jnp.sqrt(kap[lev, at, :] * wet)
                s_ref[pl.ds(pl.multiple_of(lev * PAD + 8 + xt * 8, 8), 8), :] = v
                acc = edge(acc, v, dl * 8 + xt)
        sysend[g] = acc
        return c

    lax.fori_loop(0, LEV // 8, start_s, 0)

    def edge_columns(src, dst, g, c):
        acc = jnp.zeros((8, 128), F32)
        for dl in range(4):
            lev = g * 4 + dl
            for t in range(2):
                for xt in range(XT):
                    base = (t * LEV + lev) * PAD + 8 + xt * 8
                    acc = edge(acc, src[pl.ds(pl.multiple_of(base, 8), 8), :], dl * 16 + t * 8 + xt)
        dst[g] = acc
        return c

    def start_u(g, c):
        acc = jnp.zeros((8, 128), F32)
        for dl in range(4):
            lev = g * 4 + dl
            for xt in range(XT):
                s = s_ref[pl.ds(pl.multiple_of(lev * PAD + 8 + xt * 8, 8), 8), :]
                for t in range(2):
                    u = s * tr[t, lev, xt * 8:xt * 8 + 8, :]
                    u_one[pl.ds(pl.multiple_of((t * LEV + lev) * PAD + 8 + xt * 8, 8), 8), :] = u
                    acc = edge(acc, u, dl * 16 + t * 8 + xt)
        ysend[0, g] = acc
        return c

    lax.fori_loop(0, GROUPS, start_u, 0)

    for xt in range(XT):
        at = slice(xt * 8, xt * 8 + 8)
        b_ref[at, :] = 0.05 * land[at, :].astype(F32)

    def edge_rows(src, dst, levels):
        for j in range(levels // 8):
            dst[0, j * 8:j * 8 + 8, :] = src[pl.ds(j * 8 * PAD + 8 + CX - 1, 8, stride=PAD), :]
            dst[1, j * 8:j * 8 + 8, :] = src[pl.ds(j * 8 * PAD + 8, 8, stride=PAD), :]

    def halo_rows(src, dst, levels):
        for j in range(levels // 8):
            dst[pl.ds(j * 8 * PAD + 7, 8, stride=PAD), :] = src[0, j * 8:j * 8 + 8, :]
            dst[pl.ds(j * 8 * PAD + 8 + CX, 8, stride=PAD), :] = src[1, j * 8:j * 8 + 8, :]

    def halo_copies(xs, xr, ys, yr, n):
        made = []
        for side, (dx, dy) in enumerate(((1, 0), (-1, 0), (0, 1), (0, -1))):
            src = xs.at[side] if side < 2 else ys
            dst = xr.at[side] if side < 2 else yr.at[side - 2]
            copy = pltpu.make_async_remote_copy(
                src_ref=src, dst_ref=dst, send_sem=hs_sem.at[n, side], recv_sem=hr_sem.at[n, side],
                device_id=(gx + dx, gy + dy), device_id_type=MESH)
            made.append((inside(dx, dy), inside(-dx, -dy), copy))
        return made

    def offset_copies(src, dst, ss, rs, sign):
        made = []
        for o in AROUND:
            dx, dy = OFFSETS[o][0] * sign, OFFSETS[o][1] * sign
            copy = pltpu.make_async_remote_copy(
                src_ref=src.at[o], dst_ref=dst.at[o], send_sem=ss.at[o], recv_sem=rs.at[o],
                device_id=(gx + dx, gy + dy), device_id_type=MESH)
            made.append((inside(dx, dy), inside(-dx, -dy), copy))
        return made

    def start(copies):
        for can, _, copy in copies:
            pl.when(can)(copy.start)

    def received(copies):
        for _, comes, copy in copies:
            pl.when(comes)(copy.wait_recv)

    def sent(copies):
        for can, _, copy in copies:
            pl.when(can)(copy.wait_send)

    wide = 1 + (gx > 0).astype(I32) + (gx < n_gx - 1).astype(I32)
    high = 1 + (gy > 0).astype(I32) + (gy < n_gy - 1).astype(I32)
    pl.semaphore_wait(barrier, wide * high - 1)

    packs = offset_copies(psend, precv, ps_sem, pr_sem, 1)
    start(packs)
    edge_rows(s_ref, sxsend, LEV)
    s_halos = halo_copies(sxsend, sxrecv, sysend, syrecv, STEPS)
    start(s_halos)
    edge_rows(u_one, xsend.at[0], 2 * LEV)
    u_halos = [halo_copies(xsend.at[n], xrecv.at[n], ysend.at[n], yrecv.at[n], n) for n in range(STEPS)]
    start(u_halos[0])

    def columns_in(src, groups):
        for g in range(groups):
            comb[g] = jnp.where(lane % 2 == 1, pltpu.roll(src[0, g], 1, 1), pltpu.roll(src[1, g], 127, 1))

    loads[2].wait()
    loads[3].wait()

    apart = jnp.abs(lax.broadcasted_iota(I32, (128, 128), 0) - lax.broadcasted_iota(I32, (128, 128), 1))
    near = jnp.where(apart == 1, 1.0, 0.0).astype(BF16)
    beside_s[:128] = near
    beside_s[128:] = near

    def two_parts(v):
        head = v.astype(BF16)
        return jnp.concatenate([head, (v - head.astype(F32)).astype(BF16)], 1)

    def beside(src, bases):
        blocks = [two_parts(src[pl.ds(pl.multiple_of(base, 8), CX), :]) for base in bases]
        return jnp.dot(jnp.concatenate(blocks, 0), beside_s[...], preferred_element_type=F32)

    def across(inner, packed, i):
        return inner[i * 8:i * 8 + 8] + jnp.where(at_end, pltpu.roll(packed, 127 - 2 * i, 1), 0.0)

    at_end = (lane == 0) | (lane == 127)

    received(s_halos)
    halo_rows(sxrecv, s_ref, LEV)
    columns_in(syrecv, LEV // 8)

    def centre(g, c):
        packed = comb[g]
        inner = beside(s_ref, [(g * 8 + dl) * PAD + 8 for dl in range(8)])
        for dl in range(8):
            lev = g * 8 + dl
            for xt in range(XT):
                base = lev * PAD + 8 + xt * 8
                s = s_ref[pl.ds(pl.multiple_of(base, 8), 8), :]
                total = across(inner, packed, dl * 8 + xt) + s_ref[pl.ds(base - 1, 8), :] + s_ref[pl.ds(base + 1, 8), :]
                a_ref[lev, xt * 8:xt * 8 + 8, :] = 1.0 - s * total - 2.0 * b_ref[xt * 8:xt * 8 + 8, :]
        return c

    lax.fori_loop(0, LEV // 8, centre, 0)

    def diffuse(step, c_src, c_dst, u_src, u_dst):
        received(u_halos[step])
        halo_rows(xrecv.at[step], u_src, 2 * LEV)
        columns_in(yrecv.at[step], GROUPS)

        def group(g, c):
            packed = comb[g]
            inner = beside(u_src, [(t * LEV + g * 4 + dl) * PAD + 8 for dl in range(4) for t in range(2)])
            added = jnp.minimum(g, 1)
            for dl in range(4):
                lev = g * 4 + dl
                above, below = jnp.maximum(lev - 1, 0), jnp.minimum(lev + 1, LEV - 1)
                for xt in range(XT):
                    at = slice(xt * 8, xt * 8 + 8)
                    s = s_ref[pl.ds(pl.multiple_of(lev * PAD + 8 + xt * 8, 8), 8), :]
                    a, b = a_ref[lev, at, :], b_ref[at, :]
                    for t in range(2):
                        base = (t * LEV + lev) * PAD + 8 + xt * 8
                        total = across(inner, packed, dl * 16 + t * 8 + xt) + u_src[pl.ds(base - 1, 8), :] + u_src[pl.ds(base + 1, 8), :]
                        new = a * c_src[t, lev, at, :] + s * total + b * (c_src[t, above, at, :] + c_src[t, below, at, :])
                        if dl == 0 and step > 0:
                            new = new + force[added, t, at, :]
                        c_dst[t, lev, at, :] = new
                        if step < STEPS - 1:
                            u_dst[pl.ds(pl.multiple_of(base, 8), 8), :] = s * new
            return c

        lax.fori_loop(0, GROUPS, group, 0)

    def send_halos(step, src):
        lax.fori_loop(0, GROUPS, functools.partial(edge_columns, src, ysend.at[step]), 0)
        edge_rows(src, xsend.at[step], 2 * LEV)
        start(u_halos[step])

    diffuse(0, tr, c_one, u_one, u_two)

    received(packs)

    table = jnp.concatenate([precv[h // 2, :, (h % 2) * 256:(h % 2) * 256 + 256] for h in range(18)], 0)
    head = table.astype(BF16)
    table_s[0] = head
    table_s[1] = (table - head.astype(F32)).astype(BF16)

    def gather(i, c):
        for xx in range(GX):
            x = i * GX + xx
            hot = jnp.concatenate([onehot_rows(slot[k, pl.ds(x, 1), :] & 255, 256) for k in range(K)], 1)
            found = jnp.dot(table_s[0], hot, preferred_element_type=F32) + jnp.dot(table_s[1], hot, preferred_element_type=F32)
            acc = jnp.zeros((8, 128), F32)
            for k in range(K):
                high = jnp.broadcast_to(slot[k, pl.ds(x, 1), :], (8, 128)) >> 8
                r = jnp.zeros((8, 128), F32)
                for h in range(18):
                    r = jnp.where(high == h, found[h * 8:h * 8 + 8, k * 128:k * 128 + 128], r)
                acc = acc + jnp.broadcast_to(weight[k, pl.ds(x, 1), :], (8, 128)) * r
            remap[pl.ds(pl.multiple_of(x * 8, 8), 8), :] = acc
        return c

    lax.fori_loop(0, CX // GX, gather, 0)

    for xt in range(XT):
        at = slice(xt * 8, xt * 8 + 8)
        r = [remap[pl.ds(xt * 64 + f, 8, stride=8), :] for f in range(NFIELD)]
        wet = land[at, :].astype(F32)
        ws = jnp.sqrt(r[0] * r[0] + r[1] * r[1] + 1.0)
        heat = (ws * (r[2] - tr[0, 0, at, :]) + r[4] + r[5]) * wet
        water = (ws * (r[3] - 0.2 * tr[1, 0, at, :]) - r[6]) * wet
        sx = (ws * r[0] + 0.5 * r[7]) * wet
        sy = (ws * r[1] - 0.5 * r[7]) * wet
        for g, v in enumerate((heat, water, sx, sy)):
            flux8[pl.ds(xt * 64 + g, 8, stride=8), :] = v
            flux8[pl.ds(xt * 64 + g + 4, 8, stride=8), :] = v
        for t, v in enumerate((0.05 * heat, -0.05 * water)):
            force[0, t, at, :] = v
            v = c_one[t, 0, at, :] + v
            c_one[t, 0, at, :] = v
            u_two[t * LEV * PAD + 8 + xt * 8:t * LEV * PAD + 16 + xt * 8, :] = s_ref[8 + xt * 8:16 + xt * 8, :] * v
        force[1, 0, at, :] = jnp.zeros((8, CY), F32)
        force[1, 1, at, :] = jnp.zeros((8, CY), F32)

    send_halos(1, u_two)

    def scatter_rows(i, c):
        hots, spreads = [], []
        for xx in range(SX):
            x = i * SX + xx
            for k in range(K):
                v = jnp.broadcast_to(weight[k, pl.ds(x, 1), :], (8, 128)) * flux8[pl.ds(pl.multiple_of(x * 8, 8), 8), :]
                index = slot[k, pl.ds(x, 1), :]
                hots.append(onehot_rows(index & 255, 256))
                spreads.append(spread(split_pair(v), index >> 8, 18))
        return c + lax.dot_general(
            jnp.concatenate(hots, 1), jnp.concatenate(spreads, 1), (((1,), (1,)), ((), ())), preferred_element_type=F32)

    back = lax.fori_loop(0, 2, scatter_rows, jnp.zeros((256, 144), F32))
    diffuse(1, c_one, c_two, u_two, u_one)
    send_halos(2, u_one)
    back = scatter_rows(2, back)
    diffuse(2, c_two, c_one, u_one, u_two)
    send_halos(3, u_two)
    back = scatter_rows(3, back).T
    for o in range(9):
        for half in range(2):
            h = o * 2 + half
            v = back[h * 8:h * 8 + 4] + back[h * 8 + 4:h * 8 + 8]
            if o == 4:
                bret[o, half * 4:half * 4 + 4, :] = v
            else:
                bsend[o, half * 4:half * 4 + 4, :] = v
    backs = offset_copies(bsend, bret, bs_sem, br_sem, -1)
    start(backs)

    diffuse(3, c_one, c_out, u_two, u_one)

    received(backs)
    for o in range(9):
        for q in range(4):
            half, at = q // 2, slice((q % 2) * 128, (q % 2) * 128 + 128)
            v = bret[o, :, at]
            swapped = pltpu.roll(v, 4, 0)
            first = rows((8, 128)) < 4
            v = jnp.where(first, v, swapped) if half == 0 else jnp.where(first, swapped, v)
            v = jnp.where(live(o, q * 128, 128), v, 0.0)
            index = cols[o, :, q * 128:q * 128 + 128]
            to = slice((o * 4 + q) * 128, (o * 4 + q) * 128 + 128)
            onehot_s[:, to] = onehot_rows(index & 255, 256)
            spread_s[:, to] = spread(split_pair(v), index >> 8, 8)
    ends = lax.dot_general(
        spread_s[...], onehot_s[...], (((1,), (1,)), ((), ())), preferred_element_type=F32)
    for h in range(8):
        aflux[:, h * 256:h * 256 + 256] = ends[h * 8:h * 8 + 4] + ends[h * 8 + 4:h * 8 + 8]

    sent(packs)
    sent(s_halos)
    sent(backs)
    for copies in u_halos:
        sent(copies)


def per_device(atm_fields, send_cols, pair_count, remap_slot, remap_weight, land_mask, tracers, kappa):
    V, S = pltpu.VMEM, pltpu.SemaphoreType
    hbm = pl.BlockSpec(memory_space=pl.ANY)
    return pl.pallas_call(
        kernel,
        out_shape=(
            pltpu.VMEM((4, AC), F32),
            pltpu.VMEM((2, LEV, CX, CY), F32),
        ),
        in_specs=[pl.BlockSpec(memory_space=pltpu.VMEM)] + [hbm] * 7,
        out_specs=(pl.BlockSpec(memory_space=pltpu.VMEM),) * 2,
        scratch_shapes=[
            V((8, AC), F32), V((9, 1, SLOT), I32), V((K, CX, CY), I32), V((K, CX, CY), F32), V((CX, CY), I32),
            V((2, LEV, CX, CY), F32), V((LEV, CX, CY), F32),
            V((9, 8, SLOT), F32), V((9, 8, SLOT), F32), V((9, 8, 256), F32), V((9, 8, 256), F32),
            V((CX * 8, CY), F32), V((CX * 8, CY), F32), V((2, 2, CX, CY), F32),
            V((LEV * PAD, CY), F32), V((LEV, CX, CY), F32), V((CX, CY), F32),
            V((2, LEV, CX, CY), F32), V((2, LEV, CX, CY), F32),
            V((2 * LEV * PAD, CY), F32), V((2 * LEV * PAD, CY), F32), V((GROUPS, 8, 128), F32),
            V((64, 36 * 128), BF16), V((256, 36 * 128), BF16), V((2, 144, 256), BF16), V((256, 128), BF16),
            V((STEPS, 2, 2 * LEV, CY), F32), V((STEPS, 2, 2 * LEV, CY), F32),
            V((STEPS, GROUPS, 8, 128), F32), V((STEPS, 2, GROUPS, 8, 128), F32),
            V((2, LEV, CY), F32), V((2, LEV, CY), F32), V((LEV // 8, 8, 128), F32), V((2, LEV // 8, 8, 128), F32),
            S.DMA((7,)), S.DMA((9,)), S.DMA((9,)), S.DMA((9,)), S.DMA((9,)),
            S.DMA((STEPS + 1, 4)), S.DMA((STEPS + 1, 4)),
        ],
        compiler_params=pltpu.CompilerParams(
            collective_id=0, has_side_effects=True, vmem_limit_bytes=52 << 20),
        name="couple",
    )(pair_count, atm_fields, send_cols.transpose(1, 0, 2), remap_slot, remap_weight, land_mask, tracers, kappa)


def solution(mesh):
    return jax.shard_map(
        per_device,
        mesh=mesh,
        in_specs=(
            P(None, ("gx", "gy")),
            P(("gx", "gy"), None, None),
            P(("gx", "gy"), None),
            P(None, "gx", "gy"),
            P(None, "gx", "gy"),
            P("gx", "gy"),
            P(None, None, "gx", "gy"),
            P(None, "gx", "gy"),
        ),
        out_specs=(P(None, ("gx", "gy")), P(None, None, "gx", "gy")),
        check_vma=False,
    )
```

```python
import functools

import jax
import jax.numpy as jnp
from jax import lax
from jax.experimental import pallas as pl
from jax.experimental.pallas import tpu as pltpu
from jax.sharding import PartitionSpec as P

MESH = pl.DeviceIdType.MESH
F32, BF16, I32 = jnp.float32, jnp.bfloat16, jnp.int32
NFIELD, AC, SLOT, K, CX, CY, LEV, STEPS = 8, 2048, 512, 4, 64, 128, 32, 4
OFFSETS = [(o // 3 - 1, o % 3 - 1) for o in range(9)]
AROUND = [o for o in range(9) if o != 4]
XT = CX // 8
GROUPS = LEV // 4
GX, SX = 16, 16
PAD = CX + 16


def lanes(shape):
    return lax.broadcasted_iota(I32, shape, len(shape) - 1)


def rows(shape):
    return lax.broadcasted_iota(I32, shape, len(shape) - 2)


def split_pair(v):
    head = v.astype(BF16).astype(F32)
    return jnp.where(rows(v.shape) < 4, head, v - head)


def onehot_rows(index, count):
    at = rows((count, 128)).astype(F32).astype(BF16)
    low = jnp.broadcast_to(index.astype(F32), (16, 128)).astype(BF16)
    low = jnp.concatenate([low] * (count // 16), 0)
    return jnp.where(at == low, jnp.ones((), BF16), jnp.zeros((), BF16))


def spread(pair, high, count):
    two = jnp.concatenate([pair, pair], 0).astype(BF16)
    at = (jnp.broadcast_to(high, (16, 128)) - rows((16, 128)) // 8).astype(F32).astype(BF16)
    zero = jnp.zeros((), BF16)
    return jnp.concatenate([jnp.where(at == jnp.asarray(2 * q, BF16), two, zero) for q in range(count // 2)], 0)


def kernel(
    pc_ref, atm_hbm, cols_hbm, slot_hbm, weight_hbm, land_hbm, tr_hbm, kap_hbm,
    aflux, c_out,
    atm, cols, slot, weight, land, tr, kap,
    psend, precv, bsend, bret, remap, flux8, force,
    s_ref, a_ref, b_ref, c_one, c_two, u_one, u_two, comb,
    spread_s, onehot_s, table_s, beside_s,
    xsend, xrecv, ysend, yrecv, sxsend, sxrecv, sysend, syrecv,
    in_sem, ps_sem, pr_sem, bs_sem, br_sem, hs_sem, hr_sem,
):
    gx, gy = lax.axis_index("gx"), lax.axis_index("gy")
    n_gx, n_gy = lax.axis_size("gx"), lax.axis_size("gy")

    def inside(dx, dy):
        ok = None
        for at, d, n in ((gx, dx, n_gx), (gy, dy, n_gy)):
            c = at > 0 if d < 0 else at < n - 1 if d > 0 else None
            if c is not None:
                ok = c if ok is None else ok & c
        return ok

    sources = (atm_hbm, cols_hbm, slot_hbm, weight_hbm, land_hbm, tr_hbm, kap_hbm)
    targets = (atm, cols, slot, weight, land, tr, kap)
    loads = [pltpu.make_async_copy(a, b, in_sem.at[i]) for i, (a, b) in enumerate(zip(sources, targets))]
    for i in (0, 1, 4, 6, 5, 2, 3):
        loads[i].start()

    barrier = pltpu.get_barrier_semaphore()
    for o in AROUND:
        dx, dy = OFFSETS[o]

        @pl.when(inside(dx, dy))
        def _():
            pl.semaphore_signal(barrier, inc=1, device_id=(gx + dx, gy + dy), device_id_type=MESH)

    for side, missing in ((0, gx == 0), (1, gx == n_gx - 1)):
        @pl.when(missing)
        def _():
            for step in range(STEPS):
                xrecv[step, side] = jnp.zeros((2 * LEV, CY), F32)
            sxrecv[side] = jnp.zeros((LEV, CY), F32)
    for side, missing in ((0, gy == 0), (1, gy == n_gy - 1)):
        @pl.when(missing)
        def _():
            for step in range(STEPS):
                yrecv[step, side] = jnp.zeros((GROUPS, 8, 128), F32)
            syrecv[side] = jnp.zeros((LEV // 8, 8, 128), F32)

    def live(o, base, width):
        count = jnp.broadcast_to(pc_ref[0:1, o:o + 1], (8, width))
        return lanes((8, width)) + base < count

    loads[0].wait()
    loads[1].wait()
    for o in range(9):
        for q in range(SLOT // 128):
            index = jnp.broadcast_to(cols[o, :, q * 128:q * 128 + 128], (8, 128))
            low, high = index & 127, index >> 7
            r = jnp.zeros((8, 128), F32)
            for h in range(AC // 128):
                got = jnp.take_along_axis(atm[:, h * 128:h * 128 + 128], low, axis=1, mode="promise_in_bounds")
                r = jnp.where(high == h, got, r)
            r = jnp.where(live(o, q * 128, 128), r, 0.0)
            if o == 4:
                precv[o, :, q * 128:q * 128 + 128] = r
            else:
                psend[o, :, q * 128:q * 128 + 128] = r

    def edge_rows(src, dst, levels):
        for j in range(levels // 8):
            dst[0, j * 8:j * 8 + 8, :] = src[pl.ds(j * 8 * PAD + 8 + CX - 1, 8, stride=PAD), :]
            dst[1, j * 8:j * 8 + 8, :] = src[pl.ds(j * 8 * PAD + 8, 8, stride=PAD), :]

    def halo_rows(src, dst, levels):
        for j in range(levels // 8):
            dst[pl.ds(j * 8 * PAD + 7, 8, stride=PAD), :] = src[0, j * 8:j * 8 + 8, :]
            dst[pl.ds(j * 8 * PAD + 8 + CX, 8, stride=PAD), :] = src[1, j * 8:j * 8 + 8, :]

    def halo_copies(xs, xr, ys, yr, n):
        made = []
        for side, (dx, dy) in enumerate(((1, 0), (-1, 0), (0, 1), (0, -1))):
            src = xs.at[side] if side < 2 else ys
            dst = xr.at[side] if side < 2 else yr.at[side - 2]
            copy = pltpu.make_async_remote_copy(
                src_ref=src, dst_ref=dst, send_sem=hs_sem.at[n, side], recv_sem=hr_sem.at[n, side],
                device_id=(gx + dx, gy + dy), device_id_type=MESH)
            made.append((inside(dx, dy), inside(-dx, -dy), copy))
        return made

    def offset_copies(src, dst, ss, rs, sign):
        made = []
        for o in AROUND:
            dx, dy = OFFSETS[o][0] * sign, OFFSETS[o][1] * sign
            copy = pltpu.make_async_remote_copy(
                src_ref=src.at[o], dst_ref=dst.at[o], send_sem=ss.at[o], recv_sem=rs.at[o],
                device_id=(gx + dx, gy + dy), device_id_type=MESH)
            made.append((inside(dx, dy), inside(-dx, -dy), copy))
        return made

    def start(copies):
        for can, _, copy in copies:
            pl.when(can)(copy.start)

    def received(copies):
        for _, comes, copy in copies:
            pl.when(comes)(copy.wait_recv)

    def sent(copies):
        for can, _, copy in copies:
            pl.when(can)(copy.wait_send)

    wide = 1 + (gx > 0).astype(I32) + (gx < n_gx - 1).astype(I32)
    high = 1 + (gy > 0).astype(I32) + (gy < n_gy - 1).astype(I32)
    pl.semaphore_wait(barrier, wide * high - 1)

    packs = offset_copies(psend, precv, ps_sem, pr_sem, 1)
    start(packs)
    loads[4].wait()
    loads[6].wait()
    lane = lanes((8, 128))

    def edge(acc, v, i):
        turned = pltpu.roll(v, 2 * i + 1, 1)
        return jnp.where((lane == 2 * i) | (lane == 2 * i + 1), turned, acc)

    def start_s(g, c):
        acc = jnp.zeros((8, 128), F32)
        for dl in range(8):
            lev = g * 8 + dl
            for xt in range(XT):
                at = slice(xt * 8, xt * 8 + 8)
                wet = land[at, :].astype(F32)
                v = jnp.sqrt(kap[lev, at, :] * wet)
                s_ref[pl.ds(pl.multiple_of(lev * PAD + 8 + xt * 8, 8), 8), :] = v
                acc = edge(acc, v, dl * 8 + xt)
        sysend[g] = acc
        return c

    lax.fori_loop(0, LEV // 8, start_s, 0)
    edge_rows(s_ref, sxsend, LEV)
    s_halos = halo_copies(sxsend, sxrecv, sysend, syrecv, STEPS)
    start(s_halos)

    def edge_columns(src, dst, g, c):
        acc = jnp.zeros((8, 128), F32)
        for dl in range(4):
            lev = g * 4 + dl
            for t in range(2):
                for xt in range(XT):
                    base = (t * LEV + lev) * PAD + 8 + xt * 8
                    acc = edge(acc, src[pl.ds(pl.multiple_of(base, 8), 8), :], dl * 16 + t * 8 + xt)
        dst[g] = acc
        return c

    def start_u(g, c):
        acc = jnp.zeros((8, 128), F32)
        for dl in range(4):
            lev = g * 4 + dl
            for xt in range(XT):
                s = s_ref[pl.ds(pl.multiple_of(lev * PAD + 8 + xt * 8, 8), 8), :]
                for t in range(2):
                    u = s * tr[t, lev, xt * 8:xt * 8 + 8, :]
                    u_one[pl.ds(pl.multiple_of((t * LEV + lev) * PAD + 8 + xt * 8, 8), 8), :] = u
                    acc = edge(acc, u, dl * 16 + t * 8 + xt)
        ysend[0, g] = acc
        return c

    loads[5].wait()
    lax.fori_loop(0, GROUPS, start_u, 0)

    edge_rows(u_one, xsend.at[0], 2 * LEV)
    u_halos = [halo_copies(xsend.at[n], xrecv.at[n], ysend.at[n], yrecv.at[n], n) for n in range(STEPS)]
    start(u_halos[0])

    def columns_in(src, groups):
        for g in range(groups):
            comb[g] = jnp.where(lane % 2 == 1, pltpu.roll(src[0, g], 1, 1), pltpu.roll(src[1, g], 127, 1))

    apart = jnp.abs(lax.broadcasted_iota(I32, (128, 128), 0) - lax.broadcasted_iota(I32, (128, 128), 1))
    near = jnp.where(apart == 1, 1.0, 0.0).astype(BF16)
    beside_s[:128] = near
    beside_s[128:] = near

    def two_parts(v):
        head = v.astype(BF16)
        return jnp.concatenate([head, (v - head.astype(F32)).astype(BF16)], 1)

    def beside(src, bases):
        blocks = [two_parts(src[pl.ds(pl.multiple_of(base, 8), CX), :]) for base in bases]
        return jnp.dot(jnp.concatenate(blocks, 0), beside_s[...], preferred_element_type=F32)

    def across(inner, packed, i):
        return inner[i * 8:i * 8 + 8] + jnp.where(at_end, pltpu.roll(packed, 127 - 2 * i, 1), 0.0)

    at_end = (lane == 0) | (lane == 127)

    def diffuse(step, c_src, c_dst, u_src, u_dst):
        received(u_halos[step])
        halo_rows(xrecv.at[step], u_src, 2 * LEV)
        columns_in(yrecv.at[step], GROUPS)

        def group(g, c):
            packed = comb[g]
            inner = beside(u_src, [(t * LEV + g * 4 + dl) * PAD + 8 for dl in range(4) for t in range(2)])
            added = jnp.minimum(g, 1)
            for dl in range(4):
                lev = g * 4 + dl
                above, below = jnp.maximum(lev - 1, 0), jnp.minimum(lev + 1, LEV - 1)
                for xt in range(XT):
                    at = slice(xt * 8, xt * 8 + 8)
                    s = s_ref[pl.ds(pl.multiple_of(lev * PAD + 8 + xt * 8, 8), 8), :]
                    a, b = a_ref[lev, at, :], b_ref[at, :]
                    for t in range(2):
                        base = (t * LEV + lev) * PAD + 8 + xt * 8
                        total = across(inner, packed, dl * 16 + t * 8 + xt) + u_src[pl.ds(base - 1, 8), :] + u_src[pl.ds(base + 1, 8), :]
                        new = a * c_src[t, lev, at, :] + s * total + b * (c_src[t, above, at, :] + c_src[t, below, at, :])
                        if dl == 0:
                            new = new + force[added, t, at, :]
                        c_dst[t, lev, at, :] = new
                        if step < STEPS - 1:
                            u_dst[pl.ds(pl.multiple_of(base, 8), 8), :] = s * new
            return c

        lax.fori_loop(0, GROUPS, group, 0)

    def send_halos(step, src):
        lax.fori_loop(0, GROUPS, functools.partial(edge_columns, src, ysend.at[step]), 0)
        edge_rows(src, xsend.at[step], 2 * LEV)
        start(u_halos[step])

    for xt in range(XT):
        at = slice(xt * 8, xt * 8 + 8)
        b_ref[at, :] = 0.05 * land[at, :].astype(F32)

    for o in range(9):
        for q in range(SLOT // 128):
            to = slice((o * 4 + q) * 128, (o * 4 + q) * 128 + 128)
            onehot_s[:, to] = onehot_rows(cols[o, :, q * 128:q * 128 + 128] & 255, 256)

    loads[2].wait()
    loads[3].wait()

    received(packs)

    table = jnp.concatenate([precv[h // 2, :, (h % 2) * 256:(h % 2) * 256 + 256] for h in range(18)], 0)
    head = table.astype(BF16)
    table_s[0] = head
    table_s[1] = (table - head.astype(F32)).astype(BF16)

    def gather(i, c):
        for xx in range(GX):
            x = i * GX + xx
            hot = jnp.concatenate([onehot_rows(slot[k, pl.ds(x, 1), :] & 255, 256) for k in range(K)], 1)
            found = jnp.dot(table_s[0], hot, preferred_element_type=F32) + jnp.dot(table_s[1], hot, preferred_element_type=F32)
            acc = jnp.zeros((8, 128), F32)
            for k in range(K):
                high = jnp.broadcast_to(slot[k, pl.ds(x, 1), :], (8, 128)) >> 8
                r = jnp.zeros((8, 128), F32)
                for h in range(18):
                    r = jnp.where(high == h, found[h * 8:h * 8 + 8, k * 128:k * 128 + 128], r)
                acc = acc + jnp.broadcast_to(weight[k, pl.ds(x, 1), :], (8, 128)) * r
            remap[pl.ds(pl.multiple_of(x * 8, 8), 8), :] = acc
        return c

    lax.fori_loop(0, CX // GX, gather, 0)

    for xt in range(XT):
        at = slice(xt * 8, xt * 8 + 8)
        r = [remap[pl.ds(xt * 64 + f, 8, stride=8), :] for f in range(NFIELD)]
        wet = land[at, :].astype(F32)
        ws = jnp.sqrt(r[0] * r[0] + r[1] * r[1] + 1.0)
        heat = (ws * (r[2] - tr[0, 0, at, :]) + r[4] + r[5]) * wet
        water = (ws * (r[3] - 0.2 * tr[1, 0, at, :]) - r[6]) * wet
        sx = (ws * r[0] + 0.5 * r[7]) * wet
        sy = (ws * r[1] - 0.5 * r[7]) * wet
        for g, v in enumerate((heat, water, sx, sy)):
            flux8[pl.ds(xt * 64 + g, 8, stride=8), :] = v
            flux8[pl.ds(xt * 64 + g + 4, 8, stride=8), :] = v
        force[0, 0, at, :] = 0.05 * heat
        force[0, 1, at, :] = -0.05 * water
        force[1, 0, at, :] = jnp.zeros((8, CY), F32)
        force[1, 1, at, :] = jnp.zeros((8, CY), F32)

    received(s_halos)
    halo_rows(sxrecv, s_ref, LEV)
    columns_in(syrecv, LEV // 8)

    def centre(g, c):
        packed = comb[g]
        inner = beside(s_ref, [(g * 8 + dl) * PAD + 8 for dl in range(8)])
        for dl in range(8):
            lev = g * 8 + dl
            for xt in range(XT):
                base = lev * PAD + 8 + xt * 8
                s = s_ref[pl.ds(pl.multiple_of(base, 8), 8), :]
                total = across(inner, packed, dl * 8 + xt) + s_ref[pl.ds(base - 1, 8), :] + s_ref[pl.ds(base + 1, 8), :]
                a_ref[lev, xt * 8:xt * 8 + 8, :] = 1.0 - s * total - 2.0 * b_ref[xt * 8:xt * 8 + 8, :]
        return c

    lax.fori_loop(0, LEV // 8, centre, 0)

    diffuse(0, tr, c_one, u_one, u_two)
    send_halos(1, u_two)

    def scatter_rows(i, c):
        hots, spreads = [], []
        for xx in range(SX):
            x = i * SX + xx
            for k in range(K):
                v = jnp.broadcast_to(weight[k, pl.ds(x, 1), :], (8, 128)) * flux8[pl.ds(pl.multiple_of(x * 8, 8), 8), :]
                index = slot[k, pl.ds(x, 1), :]
                hots.append(onehot_rows(index & 255, 256))
                spreads.append(spread(split_pair(v), index >> 8, 18))
        return c + lax.dot_general(
            jnp.concatenate(hots, 1), jnp.concatenate(spreads, 1), (((1,), (1,)), ((), ())), preferred_element_type=F32)

    back = lax.fori_loop(0, 2, scatter_rows, jnp.zeros((256, 144), F32))
    diffuse(1, c_one, c_two, u_two, u_one)
    send_halos(2, u_one)
    back = scatter_rows(2, back)
    diffuse(2, c_two, c_one, u_one, u_two)
    send_halos(3, u_two)
    back = scatter_rows(3, back).T
    for o in range(9):
        for half in range(2):
            h = o * 2 + half
            v = back[h * 8:h * 8 + 4] + back[h * 8 + 4:h * 8 + 8]
            if o == 4:
                bret[o, half * 4:half * 4 + 4, :] = v
            else:
                bsend[o, half * 4:half * 4 + 4, :] = v
    backs = offset_copies(bsend, bret, bs_sem, br_sem, -1)
    start(backs)

    diffuse(3, c_one, c_out, u_two, u_one)

    received(backs)
    for o in range(9):
        for q in range(4):
            half, at = q // 2, slice((q % 2) * 128, (q % 2) * 128 + 128)
            v = bret[o, :, at]
            swapped = pltpu.roll(v, 4, 0)
            first = rows((8, 128)) < 4
            v = jnp.where(first, v, swapped) if half == 0 else jnp.where(first, swapped, v)
            v = jnp.where(live(o, q * 128, 128), v, 0.0)
            index = cols[o, :, q * 128:q * 128 + 128]
            to = slice((o * 4 + q) * 128, (o * 4 + q) * 128 + 128)
            spread_s[:, to] = spread(split_pair(v), index >> 8, 8)
    ends = lax.dot_general(
        spread_s[...], onehot_s[...], (((1,), (1,)), ((), ())), preferred_element_type=F32)
    for h in range(8):
        aflux[:, h * 256:h * 256 + 256] = ends[h * 8:h * 8 + 4] + ends[h * 8 + 4:h * 8 + 8]

    sent(packs)
    sent(s_halos)
    sent(backs)
    for copies in u_halos:
        sent(copies)


def per_device(atm_fields, send_cols, pair_count, remap_slot, remap_weight, land_mask, tracers, kappa):
    V, S = pltpu.VMEM, pltpu.SemaphoreType
    hbm = pl.BlockSpec(memory_space=pl.ANY)
    return pl.pallas_call(
        kernel,
        out_shape=(
            pltpu.VMEM((4, AC), F32),
            pltpu.VMEM((2, LEV, CX, CY), F32),
        ),
        in_specs=[pl.BlockSpec(memory_space=pltpu.VMEM)] + [hbm] * 7,
        out_specs=(pl.BlockSpec(memory_space=pltpu.VMEM),) * 2,
        scratch_shapes=[
            V((8, AC), F32), V((9, 1, SLOT), I32), V((K, CX, CY), I32), V((K, CX, CY), F32), V((CX, CY), I32),
            V((2, LEV, CX, CY), F32), V((LEV, CX, CY), F32),
            V((9, 8, SLOT), F32), V((9, 8, SLOT), F32), V((9, 8, 256), F32), V((9, 8, 256), F32),
            V((CX * 8, CY), F32), V((CX * 8, CY), F32), V((2, 2, CX, CY), F32),
            V((LEV * PAD, CY), F32), V((LEV, CX, CY), F32), V((CX, CY), F32),
            V((2, LEV, CX, CY), F32), V((2, LEV, CX, CY), F32),
            V((2 * LEV * PAD, CY), F32), V((2 * LEV * PAD, CY), F32), V((GROUPS, 8, 128), F32),
            V((64, 36 * 128), BF16), V((256, 36 * 128), BF16), V((2, 144, 256), BF16), V((256, 128), BF16),
            V((STEPS, 2, 2 * LEV, CY), F32), V((STEPS, 2, 2 * LEV, CY), F32),
            V((STEPS, GROUPS, 8, 128), F32), V((STEPS, 2, GROUPS, 8, 128), F32),
            V((2, LEV, CY), F32), V((2, LEV, CY), F32), V((LEV // 8, 8, 128), F32), V((2, LEV // 8, 8, 128), F32),
            S.DMA((7,)), S.DMA((9,)), S.DMA((9,)), S.DMA((9,)), S.DMA((9,)),
            S.DMA((STEPS + 1, 4)), S.DMA((STEPS + 1, 4)),
        ],
        compiler_params=pltpu.CompilerParams(
            collective_id=0, has_side_effects=True, vmem_limit_bytes=52 << 20),
        name="couple",
    )(pair_count, atm_fields, send_cols.transpose(1, 0, 2), remap_slot, remap_weight, land_mask, tracers, kappa)


def solution(mesh):
    return jax.shard_map(
        per_device,
        mesh=mesh,
        in_specs=(
            P(None, ("gx", "gy")),
            P(("gx", "gy"), None, None),
            P(("gx", "gy"), None),
            P(None, "gx", "gy"),
            P(None, "gx", "gy"),
            P("gx", "gy"),
            P(None, None, "gx", "gy"),
            P(None, "gx", "gy"),
        ),
        out_specs=(P(None, ("gx", "gy")), P(None, None, "gx", "gy")),
        check_vma=False,
    )
```

```python
import functools

import jax
import jax.numpy as jnp
from jax import lax
from jax.experimental import pallas as pl
from jax.experimental.pallas import tpu as pltpu
from jax.sharding import PartitionSpec as P

MESH = pl.DeviceIdType.MESH
F32, BF16, I32 = jnp.float32, jnp.bfloat16, jnp.int32
NFIELD, AC, SLOT, K, CX, CY, LEV, STEPS = 8, 2048, 512, 4, 64, 128, 32, 4
OFFSETS = [(o // 3 - 1, o % 3 - 1) for o in range(9)]
AROUND = [o for o in range(9) if o != 4]
XT = CX // 8
GROUPS = LEV // 8
GX, SX = 16, 16
PAD = CX + 16


def lanes(shape):
    return lax.broadcasted_iota(I32, shape, len(shape) - 1)


def rows(shape):
    return lax.broadcasted_iota(I32, shape, len(shape) - 2)


def split_pair(v):
    head = v.astype(BF16).astype(F32)
    return jnp.where(rows(v.shape) < 4, head, v - head)


def onehot_rows(index, count):
    at = rows((count, 128)).astype(F32).astype(BF16)
    low = jnp.broadcast_to(index.astype(F32), (16, 128)).astype(BF16)
    low = jnp.concatenate([low] * (count // 16), 0)
    return jnp.where(at == low, jnp.ones((), BF16), jnp.zeros((), BF16))


def spread(pair, high, count):
    two = jnp.concatenate([pair, pair], 0).astype(BF16)
    at = (jnp.broadcast_to(high, (16, 128)) - rows((16, 128)) // 8).astype(F32).astype(BF16)
    zero = jnp.zeros((), BF16)
    return jnp.concatenate([jnp.where(at == jnp.asarray(2 * q, BF16), two, zero) for q in range(count // 2)], 0)


def kernel(
    pc_ref, atm_hbm, cols_hbm, slot_hbm, weight_hbm, land_hbm, tr_hbm, kap_hbm,
    aflux, c_out,
    atm, cols, slot, weight, land, tr, kap,
    psend, precv, bsend, bret, remap, flux8, force,
    s_ref, a_ref, b_ref, c_one, c_two, u_one, u_two, comb,
    spread_s, onehot_s, table_s, beside_s,
    xsend, xrecv, ysend, yrecv, sxsend, sxrecv, sysend, syrecv,
    in_sem, ps_sem, pr_sem, bs_sem, br_sem, hs_sem, hr_sem,
):
    gx, gy = lax.axis_index("gx"), lax.axis_index("gy")
    n_gx, n_gy = lax.axis_size("gx"), lax.axis_size("gy")

    def inside(dx, dy):
        ok = None
        for at, d, n in ((gx, dx, n_gx), (gy, dy, n_gy)):
            c = at > 0 if d < 0 else at < n - 1 if d > 0 else None
            if c is not None:
                ok = c if ok is None else ok & c
        return ok

    sources = (atm_hbm, cols_hbm, slot_hbm, weight_hbm, land_hbm, tr_hbm, kap_hbm)
    targets = (atm, cols, slot, weight, land, tr, kap)
    loads = [pltpu.make_async_copy(a, b, in_sem.at[i]) for i, (a, b) in enumerate(zip(sources, targets))]
    for i in (0, 1, 4, 6, 5, 2, 3):
        loads[i].start()

    barrier = pltpu.get_barrier_semaphore()
    for o in AROUND:
        dx, dy = OFFSETS[o]

        @pl.when(inside(dx, dy))
        def _():
            pl.semaphore_signal(barrier, inc=1, device_id=(gx + dx, gy + dy), device_id_type=MESH)

    for side, missing in ((0, gx == 0), (1, gx == n_gx - 1)):
        @pl.when(missing)
        def _():
            for step in range(STEPS):
                for t in range(2):
                    xrecv[step, t, side] = jnp.zeros((LEV, CY), F32)
            sxrecv[side] = jnp.zeros((LEV, CY), F32)
    for side, missing in ((0, gy == 0), (1, gy == n_gy - 1)):
        @pl.when(missing)
        def _():
            for step in range(STEPS):
                for t in range(2):
                    yrecv[step, t, side] = jnp.zeros((GROUPS, 8, 128), F32)
            syrecv[side] = jnp.zeros((LEV // 8, 8, 128), F32)

    def live(o, base, width):
        count = jnp.broadcast_to(pc_ref[0:1, o:o + 1], (8, width))
        return lanes((8, width)) + base < count

    loads[0].wait()
    loads[1].wait()
    for o in range(9):
        for q in range(SLOT // 128):
            index = jnp.broadcast_to(cols[o, :, q * 128:q * 128 + 128], (8, 128))
            low, high = index & 127, index >> 7
            r = jnp.zeros((8, 128), F32)
            for h in range(AC // 128):
                got = jnp.take_along_axis(atm[:, h * 128:h * 128 + 128], low, axis=1, mode="promise_in_bounds")
                r = jnp.where(high == h, got, r)
            r = jnp.where(live(o, q * 128, 128), r, 0.0)
            if o == 4:
                precv[o, :, q * 128:q * 128 + 128] = r
            else:
                psend[o, :, q * 128:q * 128 + 128] = r

    def edge_rows(src, dst, t=0):
        for j in range(LEV // 8):
            base = (t * LEV + j * 8) * PAD + 8
            dst[0, j * 8:j * 8 + 8, :] = src[pl.ds(base + CX - 1, 8, stride=PAD), :]
            dst[1, j * 8:j * 8 + 8, :] = src[pl.ds(base, 8, stride=PAD), :]

    def halo_rows(src, dst, t=0):
        for j in range(LEV // 8):
            base = (t * LEV + j * 8) * PAD + 8
            dst[pl.ds(base - 1, 8, stride=PAD), :] = src[0, j * 8:j * 8 + 8, :]
            dst[pl.ds(base + CX, 8, stride=PAD), :] = src[1, j * 8:j * 8 + 8, :]

    def halo_copies(xs, xr, ys, yr, n):
        made = []
        for side, (dx, dy) in enumerate(((1, 0), (-1, 0), (0, 1), (0, -1))):
            src = xs.at[side] if side < 2 else ys
            dst = xr.at[side] if side < 2 else yr.at[side - 2]
            copy = pltpu.make_async_remote_copy(
                src_ref=src, dst_ref=dst, send_sem=hs_sem.at[n, side], recv_sem=hr_sem.at[n, side],
                device_id=(gx + dx, gy + dy), device_id_type=MESH)
            made.append((inside(dx, dy), inside(-dx, -dy), copy))
        return made

    def offset_copies(src, dst, ss, rs, sign):
        made = []
        for o in AROUND:
            dx, dy = OFFSETS[o][0] * sign, OFFSETS[o][1] * sign
            copy = pltpu.make_async_remote_copy(
                src_ref=src.at[o], dst_ref=dst.at[o], send_sem=ss.at[o], recv_sem=rs.at[o],
                device_id=(gx + dx, gy + dy), device_id_type=MESH)
            made.append((inside(dx, dy), inside(-dx, -dy), copy))
        return made

    def start(copies):
        for can, _, copy in copies:
            pl.when(can)(copy.start)

    def received(copies):
        for _, comes, copy in copies:
            pl.when(comes)(copy.wait_recv)

    def sent(copies):
        for can, _, copy in copies:
            pl.when(can)(copy.wait_send)

    wide = 1 + (gx > 0).astype(I32) + (gx < n_gx - 1).astype(I32)
    high = 1 + (gy > 0).astype(I32) + (gy < n_gy - 1).astype(I32)
    pl.semaphore_wait(barrier, wide * high - 1)

    packs = offset_copies(psend, precv, ps_sem, pr_sem, 1)
    start(packs)
    loads[4].wait()
    loads[6].wait()
    lane = lanes((8, 128))

    def edge(acc, v, i):
        turned = pltpu.roll(v, 2 * i + 1, 1)
        return jnp.where((lane == 2 * i) | (lane == 2 * i + 1), turned, acc)

    def start_s(g, c):
        acc = jnp.zeros((8, 128), F32)
        for dl in range(8):
            lev = g * 8 + dl
            for xt in range(XT):
                at = slice(xt * 8, xt * 8 + 8)
                wet = land[at, :].astype(F32)
                v = jnp.sqrt(kap[lev, at, :] * wet)
                s_ref[pl.ds(pl.multiple_of(lev * PAD + 8 + xt * 8, 8), 8), :] = v
                acc = edge(acc, v, dl * 8 + xt)
        sysend[g] = acc
        return c

    lax.fori_loop(0, LEV // 8, start_s, 0)
    edge_rows(s_ref, sxsend)
    s_halos = halo_copies(sxsend, sxrecv, sysend, syrecv, 2 * STEPS)
    start(s_halos)

    def edge_columns(src, t, dst, g, c):
        acc = jnp.zeros((8, 128), F32)
        for dl in range(8):
            lev = g * 8 + dl
            for xt in range(XT):
                base = (t * LEV + lev) * PAD + 8 + xt * 8
                acc = edge(acc, src[pl.ds(pl.multiple_of(base, 8), 8), :], dl * 8 + xt)
        dst[g] = acc
        return c

    def start_u(t, g, c):
        acc = jnp.zeros((8, 128), F32)
        for dl in range(8):
            lev = g * 8 + dl
            for xt in range(XT):
                s = s_ref[pl.ds(pl.multiple_of(lev * PAD + 8 + xt * 8, 8), 8), :]
                u = s * tr[t, lev, xt * 8:xt * 8 + 8, :]
                u_one[pl.ds(pl.multiple_of((t * LEV + lev) * PAD + 8 + xt * 8, 8), 8), :] = u
                acc = edge(acc, u, dl * 8 + xt)
        ysend[0, t, g] = acc
        return c

    u_halos = [
        [halo_copies(xsend.at[n, t], xrecv.at[n, t], ysend.at[n, t], yrecv.at[n, t], 2 * n + t) for t in range(2)]
        for n in range(STEPS)]
    loads[5].wait()
    for t in range(2):
        lax.fori_loop(0, GROUPS, functools.partial(start_u, t), 0)
        edge_rows(u_one, xsend.at[0, t], t)
        start(u_halos[0][t])

    def columns_in(src, groups):
        for g in range(groups):
            comb[g] = jnp.where(lane % 2 == 1, pltpu.roll(src[0, g], 1, 1), pltpu.roll(src[1, g], 127, 1))

    apart = jnp.abs(lax.broadcasted_iota(I32, (128, 128), 0) - lax.broadcasted_iota(I32, (128, 128), 1))
    near = jnp.where(apart == 1, 1.0, 0.0).astype(BF16)
    beside_s[:128] = near
    beside_s[128:] = near

    def two_parts(v):
        head = v.astype(BF16)
        return jnp.concatenate([head, (v - head.astype(F32)).astype(BF16)], 1)

    def beside(src, bases):
        blocks = [two_parts(src[pl.ds(pl.multiple_of(base, 8), CX), :]) for base in bases]
        return jnp.dot(jnp.concatenate(blocks, 0), beside_s[...], preferred_element_type=F32)

    def across(inner, packed, i):
        return inner[i * 8:i * 8 + 8] + jnp.where(at_end, pltpu.roll(packed, 127 - 2 * i, 1), 0.0)

    at_end = (lane == 0) | (lane == 127)

    def diffuse_one(step, t, c_src, c_dst, u_src, u_dst):
        received(u_halos[step][t])
        halo_rows(xrecv.at[step, t], u_src, t)
        columns_in(yrecv.at[step, t], GROUPS)
        last = step == STEPS - 1

        def group(g, c):
            packed = comb[g]
            inner = beside(u_src, [(t * LEV + g * 8 + dl) * PAD + 8 for dl in range(8)])
            added = jnp.minimum(g, 1)
            for dl in range(8):
                lev = g * 8 + dl
                above, below = jnp.maximum(lev - 1, 0), jnp.minimum(lev + 1, LEV - 1)
                for xt in range(XT):
                    at = slice(xt * 8, xt * 8 + 8)
                    s = s_ref[pl.ds(pl.multiple_of(lev * PAD + 8 + xt * 8, 8), 8), :]
                    base = (t * LEV + lev) * PAD + 8 + xt * 8
                    total = across(inner, packed, dl * 8 + xt) + u_src[pl.ds(base - 1, 8), :] + u_src[pl.ds(base + 1, 8), :]
                    new = a_ref[lev, at, :] * c_src[t, lev, at, :] + s * total
                    new = new + b_ref[at, :] * (c_src[t, above, at, :] + c_src[t, below, at, :])
                    if dl == 0:
                        new = new + force[added, t, at, :]
                    c_dst[t, lev, at, :] = new
                    if not last:
                        u_dst[pl.ds(pl.multiple_of(base, 8), 8), :] = s * new
            return c

        lax.fori_loop(0, GROUPS, group, 0)
        if not last:
            lax.fori_loop(0, GROUPS, functools.partial(edge_columns, u_dst, t, ysend.at[step + 1, t]), 0)
            edge_rows(u_dst, xsend.at[step + 1, t], t)
            start(u_halos[step + 1][t])

    def diffuse(*step):
        for t in range(2):
            diffuse_one(step[0], t, *step[1:])

    for xt in range(XT):
        at = slice(xt * 8, xt * 8 + 8)
        b_ref[at, :] = 0.05 * land[at, :].astype(F32)

    for o in range(9):
        for q in range(SLOT // 128):
            to = slice((o * 4 + q) * 128, (o * 4 + q) * 128 + 128)
            onehot_s[:, to] = onehot_rows(cols[o, :, q * 128:q * 128 + 128] & 255, 256)

    loads[2].wait()
    loads[3].wait()

    received(packs)

    table = jnp.concatenate([precv[h // 2, :, (h % 2) * 256:(h % 2) * 256 + 256] for h in range(18)], 0)
    head = table.astype(BF16)
    table_s[0] = head
    table_s[1] = (table - head.astype(F32)).astype(BF16)

    def gather(i, c):
        for xx in range(GX):
            x = i * GX + xx
            hot = jnp.concatenate([onehot_rows(slot[k, pl.ds(x, 1), :] & 255, 256) for k in range(K)], 1)
            found = jnp.dot(table_s[0], hot, preferred_element_type=F32) + jnp.dot(table_s[1], hot, preferred_element_type=F32)
            acc = jnp.zeros((8, 128), F32)
            for k in range(K):
                high = jnp.broadcast_to(slot[k, pl.ds(x, 1), :], (8, 128)) >> 8
                r = jnp.zeros((8, 128), F32)
                for h in range(18):
                    r = jnp.where(high == h, found[h * 8:h * 8 + 8, k * 128:k * 128 + 128], r)
                acc = acc + jnp.broadcast_to(weight[k, pl.ds(x, 1), :], (8, 128)) * r
            remap[pl.ds(pl.multiple_of(x * 8, 8), 8), :] = acc
        return c

    lax.fori_loop(0, CX // GX, gather, 0)

    for xt in range(XT):
        at = slice(xt * 8, xt * 8 + 8)
        r = [remap[pl.ds(xt * 64 + f, 8, stride=8), :] for f in range(NFIELD)]
        wet = land[at, :].astype(F32)
        ws = jnp.sqrt(r[0] * r[0] + r[1] * r[1] + 1.0)
        heat = (ws * (r[2] - tr[0, 0, at, :]) + r[4] + r[5]) * wet
        water = (ws * (r[3] - 0.2 * tr[1, 0, at, :]) - r[6]) * wet
        sx = (ws * r[0] + 0.5 * r[7]) * wet
        sy = (ws * r[1] - 0.5 * r[7]) * wet
        for g, v in enumerate((heat, water, sx, sy)):
            flux8[pl.ds(xt * 64 + g, 8, stride=8), :] = v
            flux8[pl.ds(xt * 64 + g + 4, 8, stride=8), :] = v
        force[0, 0, at, :] = 0.05 * heat
        force[0, 1, at, :] = -0.05 * water
        force[1, 0, at, :] = jnp.zeros((8, CY), F32)
        force[1, 1, at, :] = jnp.zeros((8, CY), F32)

    received(s_halos)
    halo_rows(sxrecv, s_ref)
    columns_in(syrecv, LEV // 8)

    def centre(g, c):
        packed = comb[g]
        inner = beside(s_ref, [(g * 8 + dl) * PAD + 8 for dl in range(8)])
        for dl in range(8):
            lev = g * 8 + dl
            for xt in range(XT):
                base = lev * PAD + 8 + xt * 8
                s = s_ref[pl.ds(pl.multiple_of(base, 8), 8), :]
                total = across(inner, packed, dl * 8 + xt) + s_ref[pl.ds(base - 1, 8), :] + s_ref[pl.ds(base + 1, 8), :]
                a_ref[lev, xt * 8:xt * 8 + 8, :] = 1.0 - s * total - 2.0 * b_ref[xt * 8:xt * 8 + 8, :]
        return c

    lax.fori_loop(0, LEV // 8, centre, 0)

    diffuse(0, tr, c_one, u_one, u_two)

    def scatter_rows(i, c):
        hots, spreads = [], []
        for xx in range(SX):
            x = i * SX + xx
            for k in range(K):
                v = jnp.broadcast_to(weight[k, pl.ds(x, 1), :], (8, 128)) * flux8[pl.ds(pl.multiple_of(x * 8, 8), 8), :]
                index = slot[k, pl.ds(x, 1), :]
                hots.append(onehot_rows(index & 255, 256))
                spreads.append(spread(split_pair(v), index >> 8, 18))
        return c + lax.dot_general(
            jnp.concatenate(hots, 1), jnp.concatenate(spreads, 1), (((1,), (1,)), ((), ())), preferred_element_type=F32)

    back = lax.fori_loop(0, 2, scatter_rows, jnp.zeros((256, 144), F32))
    diffuse(1, c_one, c_two, u_two, u_one)
    back = scatter_rows(2, back)
    diffuse(2, c_two, c_one, u_one, u_two)
    back = scatter_rows(3, back).T
    for o in range(9):
        for half in range(2):
            h = o * 2 + half
            v = back[h * 8:h * 8 + 4] + back[h * 8 + 4:h * 8 + 8]
            if o == 4:
                bret[o, half * 4:half * 4 + 4, :] = v
            else:
                bsend[o, half * 4:half * 4 + 4, :] = v
    backs = offset_copies(bsend, bret, bs_sem, br_sem, -1)
    start(backs)

    diffuse(3, c_one, c_out, u_two, u_one)

    received(backs)
    for o in range(9):
        for q in range(4):
            half, at = q // 2, slice((q % 2) * 128, (q % 2) * 128 + 128)
            v = bret[o, :, at]
            swapped = pltpu.roll(v, 4, 0)
            first = rows((8, 128)) < 4
            v = jnp.where(first, v, swapped) if half == 0 else jnp.where(first, swapped, v)
            v = jnp.where(live(o, q * 128, 128), v, 0.0)
            index = cols[o, :, q * 128:q * 128 + 128]
            to = slice((o * 4 + q) * 128, (o * 4 + q) * 128 + 128)
            spread_s[:, to] = spread(split_pair(v), index >> 8, 8)
    ends = lax.dot_general(
        spread_s[...], onehot_s[...], (((1,), (1,)), ((), ())), preferred_element_type=F32)
    for h in range(8):
        aflux[:, h * 256:h * 256 + 256] = ends[h * 8:h * 8 + 4] + ends[h * 8 + 4:h * 8 + 8]

    sent(packs)
    sent(s_halos)
    sent(backs)
    for pair in u_halos:
        for copies in pair:
            sent(copies)


def per_device(atm_fields, send_cols, pair_count, remap_slot, remap_weight, land_mask, tracers, kappa):
    V, S = pltpu.VMEM, pltpu.SemaphoreType
    hbm = pl.BlockSpec(memory_space=pl.ANY)
    return pl.pallas_call(
        kernel,
        out_shape=(
            pltpu.VMEM((4, AC), F32),
            pltpu.VMEM((2, LEV, CX, CY), F32),
        ),
        in_specs=[pl.BlockSpec(memory_space=pltpu.VMEM)] + [hbm] * 7,
        out_specs=(pl.BlockSpec(memory_space=pltpu.VMEM),) * 2,
        scratch_shapes=[
            V((8, AC), F32), V((9, 1, SLOT), I32), V((K, CX, CY), I32), V((K, CX, CY), F32), V((CX, CY), I32),
            V((2, LEV, CX, CY), F32), V((LEV, CX, CY), F32),
            V((9, 8, SLOT), F32), V((9, 8, SLOT), F32), V((9, 8, 256), F32), V((9, 8, 256), F32),
            V((CX * 8, CY), F32), V((CX * 8, CY), F32), V((2, 2, CX, CY), F32),
            V((LEV * PAD, CY), F32), V((LEV, CX, CY), F32), V((CX, CY), F32),
            V((2, LEV, CX, CY), F32), V((2, LEV, CX, CY), F32),
            V((2 * LEV * PAD, CY), F32), V((2 * LEV * PAD, CY), F32), V((GROUPS, 8, 128), F32),
            V((64, 36 * 128), BF16), V((256, 36 * 128), BF16), V((2, 144, 256), BF16), V((256, 128), BF16),
            V((STEPS, 2, 2, LEV, CY), F32), V((STEPS, 2, 2, LEV, CY), F32),
            V((STEPS, 2, GROUPS, 8, 128), F32), V((STEPS, 2, 2, GROUPS, 8, 128), F32),
            V((2, LEV, CY), F32), V((2, LEV, CY), F32), V((LEV // 8, 8, 128), F32), V((2, LEV // 8, 8, 128), F32),
            S.DMA((7,)), S.DMA((9,)), S.DMA((9,)), S.DMA((9,)), S.DMA((9,)),
            S.DMA((2 * STEPS + 1, 4)), S.DMA((2 * STEPS + 1, 4)),
        ],
        compiler_params=pltpu.CompilerParams(
            collective_id=0, has_side_effects=True, vmem_limit_bytes=52 << 20),
        name="couple",
    )(pair_count, atm_fields, send_cols.transpose(1, 0, 2), remap_slot, remap_weight, land_mask, tracers, kappa)


def solution(mesh):
    return jax.shard_map(
        per_device,
        mesh=mesh,
        in_specs=(
            P(None, ("gx", "gy")),
            P(("gx", "gy"), None, None),
            P(("gx", "gy"), None),
            P(None, "gx", "gy"),
            P(None, "gx", "gy"),
            P("gx", "gy"),
            P(None, None, "gx", "gy"),
            P(None, "gx", "gy"),
        ),
        out_specs=(P(None, ("gx", "gy")), P(None, None, "gx", "gy")),
        check_vma=False,
    )
```

```python
import functools

import jax
import jax.numpy as jnp
from jax import lax
from jax.experimental import pallas as pl
from jax.experimental.pallas import tpu as pltpu
from jax.sharding import PartitionSpec as P

MESH = pl.DeviceIdType.MESH
F32, BF16, I32 = jnp.float32, jnp.bfloat16, jnp.int32
NFIELD, AC, SLOT, K, CX, CY, LEV, STEPS = 8, 2048, 512, 4, 64, 128, 32, 4
OFFSETS = [(o // 3 - 1, o % 3 - 1) for o in range(9)]
AROUND = [o for o in range(9) if o != 4]
XT = CX // 8
GROUPS = LEV // 8
GX, LOOK, SX = 16, 4, 16
PAD = CX + 16


def lanes(shape):
    return lax.broadcasted_iota(I32, shape, len(shape) - 1)


def rows(shape):
    return lax.broadcasted_iota(I32, shape, len(shape) - 2)


def split_pair(v):
    head = v.astype(BF16).astype(F32)
    return jnp.where(rows(v.shape) < 4, head, v - head)


def onehot_rows(index, count):
    at = rows((count, 128)).astype(F32).astype(BF16)
    low = jnp.broadcast_to(index.astype(F32), (16, 128)).astype(BF16)
    low = jnp.concatenate([low] * (count // 16), 0)
    return jnp.where(at == low, jnp.ones((), BF16), jnp.zeros((), BF16))


def spread(pair, high, count):
    two = jnp.concatenate([pair, pair], 0).astype(BF16)
    at = (jnp.broadcast_to(high, (16, 128)) - rows((16, 128)) // 8).astype(F32).astype(BF16)
    zero = jnp.zeros((), BF16)
    return jnp.concatenate([jnp.where(at == jnp.asarray(2 * q, BF16), two, zero) for q in range(count // 2)], 0)


def kernel(
    pc_ref, atm_hbm, cols_hbm, slot_hbm, weight_hbm, land_hbm, tr_hbm, kap_hbm,
    aflux, c_out,
    atm, cols, slot, weight, land, tr, kap,
    psend, precv, bsend, bret, remap, flux8, force,
    s_ref, a_ref, b_ref, c_one, c_two, u_one, u_two, comb,
    spread_s, onehot_s, table_s, beside_s,
    xsend, xrecv, ysend, yrecv, sxsend, sxrecv, sysend, syrecv,
    in_sem, ps_sem, pr_sem, bs_sem, br_sem, hs_sem, hr_sem,
):
    gx, gy = lax.axis_index("gx"), lax.axis_index("gy")
    n_gx, n_gy = lax.axis_size("gx"), lax.axis_size("gy")

    def inside(dx, dy):
        ok = None
        for at, d, n in ((gx, dx, n_gx), (gy, dy, n_gy)):
            c = at > 0 if d < 0 else at < n - 1 if d > 0 else None
            if c is not None:
                ok = c if ok is None else ok & c
        return ok

    sources = (atm_hbm, cols_hbm, slot_hbm, weight_hbm, land_hbm, tr_hbm, kap_hbm)
    targets = (atm, cols, slot, weight, land, tr, kap)
    loads = [pltpu.make_async_copy(a, b, in_sem.at[i]) for i, (a, b) in enumerate(zip(sources, targets))]
    for i in (0, 1, 4, 6, 5, 2, 3):
        loads[i].start()

    barrier = pltpu.get_barrier_semaphore()
    for o in AROUND:
        dx, dy = OFFSETS[o]

        @pl.when(inside(dx, dy))
        def _():
            pl.semaphore_signal(barrier, inc=1, device_id=(gx + dx, gy + dy), device_id_type=MESH)

    for side, missing in ((0, gx == 0), (1, gx == n_gx - 1)):
        @pl.when(missing)
        def _():
            for step in range(STEPS):
                for t in range(2):
                    xrecv[step, t, side] = jnp.zeros((LEV, CY), F32)
            sxrecv[side] = jnp.zeros((LEV, CY), F32)
    for side, missing in ((0, gy == 0), (1, gy == n_gy - 1)):
        @pl.when(missing)
        def _():
            for step in range(STEPS):
                for t in range(2):
                    yrecv[step, t, side] = jnp.zeros((GROUPS, 8, 128), F32)
            syrecv[side] = jnp.zeros((LEV // 8, 8, 128), F32)

    def live(o, base, width):
        count = jnp.broadcast_to(pc_ref[0:1, o:o + 1], (8, width))
        return lanes((8, width)) + base < count

    loads[0].wait()
    loads[1].wait()
    for o in range(9):
        for q in range(SLOT // 128):
            index = jnp.broadcast_to(cols[o, :, q * 128:q * 128 + 128], (8, 128))
            low, high = index & 127, index >> 7
            r = jnp.zeros((8, 128), F32)
            for h in range(AC // 128):
                got = jnp.take_along_axis(atm[:, h * 128:h * 128 + 128], low, axis=1, mode="promise_in_bounds")
                r = jnp.where(high == h, got, r)
            r = jnp.where(live(o, q * 128, 128), r, 0.0)
            if o == 4:
                precv[o, :, q * 128:q * 128 + 128] = r
            else:
                psend[o, :, q * 128:q * 128 + 128] = r

    def edge_rows(src, dst, t=0):
        for j in range(LEV // 8):
            base = (t * LEV + j * 8) * PAD + 8
            dst[0, j * 8:j * 8 + 8, :] = src[pl.ds(base + CX - 1, 8, stride=PAD), :]
            dst[1, j * 8:j * 8 + 8, :] = src[pl.ds(base, 8, stride=PAD), :]

    def halo_rows(src, dst, t=0):
        for j in range(LEV // 8):
            base = (t * LEV + j * 8) * PAD + 8
            dst[pl.ds(base - 1, 8, stride=PAD), :] = src[0, j * 8:j * 8 + 8, :]
            dst[pl.ds(base + CX, 8, stride=PAD), :] = src[1, j * 8:j * 8 + 8, :]

    def halo_copies(xs, xr, ys, yr, n):
        made = []
        for side, (dx, dy) in enumerate(((1, 0), (-1, 0), (0, 1), (0, -1))):
            src = xs.at[side] if side < 2 else ys
            dst = xr.at[side] if side < 2 else yr.at[side - 2]
            copy = pltpu.make_async_remote_copy(
                src_ref=src, dst_ref=dst, send_sem=hs_sem.at[n, side], recv_sem=hr_sem.at[n, side],
                device_id=(gx + dx, gy + dy), device_id_type=MESH)
            made.append((inside(dx, dy), inside(-dx, -dy), copy))
        return made

    def offset_copies(src, dst, ss, rs, sign):
        made = []
        for o in AROUND:
            dx, dy = OFFSETS[o][0] * sign, OFFSETS[o][1] * sign
            copy = pltpu.make_async_remote_copy(
                src_ref=src.at[o], dst_ref=dst.at[o], send_sem=ss.at[o], recv_sem=rs.at[o],
                device_id=(gx + dx, gy + dy), device_id_type=MESH)
            made.append((inside(dx, dy), inside(-dx, -dy), copy))
        return made

    def start(copies):
        for can, _, copy in copies:
            pl.when(can)(copy.start)

    def received(copies):
        for _, comes, copy in copies:
            pl.when(comes)(copy.wait_recv)

    def sent(copies):
        for can, _, copy in copies:
            pl.when(can)(copy.wait_send)

    wide = 1 + (gx > 0).astype(I32) + (gx < n_gx - 1).astype(I32)
    high = 1 + (gy > 0).astype(I32) + (gy < n_gy - 1).astype(I32)
    pl.semaphore_wait(barrier, wide * high - 1)

    packs = offset_copies(psend, precv, ps_sem, pr_sem, 1)
    start(packs)
    loads[4].wait()
    loads[6].wait()
    lane = lanes((8, 128))

    def edge(acc, v, i):
        turned = pltpu.roll(v, 2 * i + 1, 1)
        return jnp.where((lane == 2 * i) | (lane == 2 * i + 1), turned, acc)

    def start_s(g, c):
        acc = jnp.zeros((8, 128), F32)
        for dl in range(8):
            lev = g * 8 + dl
            for xt in range(XT):
                at = slice(xt * 8, xt * 8 + 8)
                wet = land[at, :].astype(F32)
                v = jnp.sqrt(kap[lev, at, :] * wet)
                s_ref[pl.ds(pl.multiple_of(lev * PAD + 8 + xt * 8, 8), 8), :] = v
                acc = edge(acc, v, dl * 8 + xt)
        sysend[g] = acc
        return c

    lax.fori_loop(0, LEV // 8, start_s, 0)
    edge_rows(s_ref, sxsend)
    s_halos = halo_copies(sxsend, sxrecv, sysend, syrecv, 2 * STEPS)
    start(s_halos)

    def edge_columns(src, t, dst, g, c):
        acc = jnp.zeros((8, 128), F32)
        for dl in range(8):
            lev = g * 8 + dl
            for xt in range(XT):
                base = (t * LEV + lev) * PAD + 8 + xt * 8
                acc = edge(acc, src[pl.ds(pl.multiple_of(base, 8), 8), :], dl * 8 + xt)
        dst[g] = acc
        return c

    def start_u(t, g, c):
        acc = jnp.zeros((8, 128), F32)
        for dl in range(8):
            lev = g * 8 + dl
            for xt in range(XT):
                s = s_ref[pl.ds(pl.multiple_of(lev * PAD + 8 + xt * 8, 8), 8), :]
                u = s * tr[t, lev, xt * 8:xt * 8 + 8, :]
                u_one[pl.ds(pl.multiple_of((t * LEV + lev) * PAD + 8 + xt * 8, 8), 8), :] = u
                acc = edge(acc, u, dl * 8 + xt)
        ysend[0, t, g] = acc
        return c

    u_halos = [
        [halo_copies(xsend.at[n, t], xrecv.at[n, t], ysend.at[n, t], yrecv.at[n, t], 2 * n + t) for t in range(2)]
        for n in range(STEPS)]
    loads[5].wait()
    for t in range(2):
        lax.fori_loop(0, GROUPS, functools.partial(start_u, t), 0)
        edge_rows(u_one, xsend.at[0, t], t)
        start(u_halos[0][t])

    def columns_in(src, groups):
        for g in range(groups):
            comb[g] = jnp.where(lane % 2 == 1, pltpu.roll(src[0, g], 1, 1), pltpu.roll(src[1, g], 127, 1))

    apart = jnp.abs(lax.broadcasted_iota(I32, (128, 128), 0) - lax.broadcasted_iota(I32, (128, 128), 1))
    near = jnp.where(apart == 1, 1.0, 0.0).astype(BF16)
    beside_s[:128] = near
    beside_s[128:] = near

    def two_parts(v):
        head = v.astype(BF16)
        return jnp.concatenate([head, (v - head.astype(F32)).astype(BF16)], 1)

    def beside(src, bases):
        blocks = [two_parts(src[pl.ds(pl.multiple_of(base, 8), CX), :]) for base in bases]
        return jnp.dot(jnp.concatenate(blocks, 0), beside_s[...], preferred_element_type=F32)

    def across(inner, packed, i):
        return inner[i * 8:i * 8 + 8] + jnp.where(at_end, pltpu.roll(packed, 127 - 2 * i, 1), 0.0)

    at_end = (lane == 0) | (lane == 127)

    def diffuse_one(step, t, c_src, c_dst, u_src, u_dst):
        received(u_halos[step][t])
        halo_rows(xrecv.at[step, t], u_src, t)
        columns_in(yrecv.at[step, t], GROUPS)
        last = step == STEPS - 1

        def group(g, c):
            packed = comb[g]
            inner = beside(u_src, [(t * LEV + g * 8 + dl) * PAD + 8 for dl in range(8)])
            added = jnp.minimum(g, 1)
            for dl in range(8):
                lev = g * 8 + dl
                above, below = jnp.maximum(lev - 1, 0), jnp.minimum(lev + 1, LEV - 1)
                for xt in range(XT):
                    at = slice(xt * 8, xt * 8 + 8)
                    s = s_ref[pl.ds(pl.multiple_of(lev * PAD + 8 + xt * 8, 8), 8), :]
                    base = (t * LEV + lev) * PAD + 8 + xt * 8
                    total = across(inner, packed, dl * 8 + xt) + u_src[pl.ds(base - 1, 8), :] + u_src[pl.ds(base + 1, 8), :]
                    new = a_ref[lev, at, :] * c_src[t, lev, at, :] + s * total
                    new = new + b_ref[at, :] * (c_src[t, above, at, :] + c_src[t, below, at, :])
                    if dl == 0:
                        new = new + force[added, t, at, :]
                    c_dst[t, lev, at, :] = new
                    if not last:
                        u_dst[pl.ds(pl.multiple_of(base, 8), 8), :] = s * new
            return c

        lax.fori_loop(0, GROUPS, group, 0)
        if not last:
            lax.fori_loop(0, GROUPS, functools.partial(edge_columns, u_dst, t, ysend.at[step + 1, t]), 0)
            edge_rows(u_dst, xsend.at[step + 1, t], t)
            start(u_halos[step + 1][t])

    def diffuse(*step):
        for t in range(2):
            diffuse_one(step[0], t, *step[1:])

    for xt in range(XT):
        at = slice(xt * 8, xt * 8 + 8)
        b_ref[at, :] = 0.05 * land[at, :].astype(F32)

    for o in range(9):
        for q in range(SLOT // 128):
            to = slice((o * 4 + q) * 128, (o * 4 + q) * 128 + 128)
            onehot_s[:, to] = onehot_rows(cols[o, :, q * 128:q * 128 + 128] & 255, 256)

    loads[2].wait()
    loads[3].wait()

    received(packs)

    table = jnp.concatenate([precv[h // 2, :, (h % 2) * 256:(h % 2) * 256 + 256] for h in range(18)], 0)
    head = table.astype(BF16)
    table_s[0] = head
    table_s[1] = (table - head.astype(F32)).astype(BF16)

    def looked_up(x):
        acc = jnp.zeros((8, 128), F32)
        for k in range(K):
            index = jnp.broadcast_to(slot[k, pl.ds(x, 1), :], (8, 128))
            low, high = index & 127, index >> 7
            r = jnp.zeros((8, 128), F32)
            for h in range(36):
                part = precv[h // 4, :, h % 4 * 128:h % 4 * 128 + 128]
                r = jnp.where(high == h, jnp.take_along_axis(part, low, axis=1, mode="promise_in_bounds"), r)
            acc = acc + jnp.broadcast_to(weight[k, pl.ds(x, 1), :], (8, 128)) * r
        remap[pl.ds(pl.multiple_of(x * 8, 8), 8), :] = acc

    def gather(i, c):
        for xx in range(GX):
            x = i * GX + xx
            if xx % (GX // LOOK) == 1:
                looked_up(x)
                continue
            hot = jnp.concatenate([onehot_rows(slot[k, pl.ds(x, 1), :] & 255, 256) for k in range(K)], 1)
            found = jnp.dot(table_s[0], hot, preferred_element_type=F32) + jnp.dot(table_s[1], hot, preferred_element_type=F32)
            acc = jnp.zeros((8, 128), F32)
            for k in range(K):
                high = jnp.broadcast_to(slot[k, pl.ds(x, 1), :], (8, 128)) >> 8
                r = jnp.zeros((8, 128), F32)
                for h in range(18):
                    r = jnp.where(high == h, found[h * 8:h * 8 + 8, k * 128:k * 128 + 128], r)
                acc = acc + jnp.broadcast_to(weight[k, pl.ds(x, 1), :], (8, 128)) * r
            remap[pl.ds(pl.multiple_of(x * 8, 8), 8), :] = acc
        return c

    lax.fori_loop(0, CX // GX, gather, 0)

    for xt in range(XT):
        at = slice(xt * 8, xt * 8 + 8)
        r = [remap[pl.ds(xt * 64 + f, 8, stride=8), :] for f in range(NFIELD)]
        wet = land[at, :].astype(F32)
        ws = jnp.sqrt(r[0] * r[0] + r[1] * r[1] + 1.0)
        heat = (ws * (r[2] - tr[0, 0, at, :]) + r[4] + r[5]) * wet
        water = (ws * (r[3] - 0.2 * tr[1, 0, at, :]) - r[6]) * wet
        sx = (ws * r[0] + 0.5 * r[7]) * wet
        sy = (ws * r[1] - 0.5 * r[7]) * wet
        for g, v in enumerate((heat, water, sx, sy)):
            flux8[pl.ds(xt * 64 + g, 8, stride=8), :] = v
            flux8[pl.ds(xt * 64 + g + 4, 8, stride=8), :] = v
        force[0, 0, at, :] = 0.05 * heat
        force[0, 1, at, :] = -0.05 * water
        force[1, 0, at, :] = jnp.zeros((8, CY), F32)
        force[1, 1, at, :] = jnp.zeros((8, CY), F32)

    received(s_halos)
    halo_rows(sxrecv, s_ref)
    columns_in(syrecv, LEV // 8)

    def centre(g, c):
        packed = comb[g]
        inner = beside(s_ref, [(g * 8 + dl) * PAD + 8 for dl in range(8)])
        for dl in range(8):
            lev = g * 8 + dl
            for xt in range(XT):
                base = lev * PAD + 8 + xt * 8
                s = s_ref[pl.ds(pl.multiple_of(base, 8), 8), :]
                total = across(inner, packed, dl * 8 + xt) + s_ref[pl.ds(base - 1, 8), :] + s_ref[pl.ds(base + 1, 8), :]
                a_ref[lev, xt * 8:xt * 8 + 8, :] = 1.0 - s * total - 2.0 * b_ref[xt * 8:xt * 8 + 8, :]
        return c

    lax.fori_loop(0, LEV // 8, centre, 0)

    diffuse(0, tr, c_one, u_one, u_two)

    def scatter_rows(i, c):
        hots, spreads = [], []
        for xx in range(SX):
            x = i * SX + xx
            for k in range(K):
                v = jnp.broadcast_to(weight[k, pl.ds(x, 1), :], (8, 128)) * flux8[pl.ds(pl.multiple_of(x * 8, 8), 8), :]
                index = slot[k, pl.ds(x, 1), :]
                hots.append(onehot_rows(index & 255, 256))
                spreads.append(spread(split_pair(v), index >> 8, 18))
        return c + lax.dot_general(
            jnp.concatenate(hots, 1), jnp.concatenate(spreads, 1), (((1,), (1,)), ((), ())), preferred_element_type=F32)

    back = lax.fori_loop(0, 2, scatter_rows, jnp.zeros((256, 144), F32))
    diffuse(1, c_one, c_two, u_two, u_one)
    back = scatter_rows(2, back)
    diffuse(2, c_two, c_one, u_one, u_two)
    back = scatter_rows(3, back).T
    for o in range(9):
        for half in range(2):
            h = o * 2 + half
            v = back[h * 8:h * 8 + 4] + back[h * 8 + 4:h * 8 + 8]
            if o == 4:
                bret[o, half * 4:half * 4 + 4, :] = v
            else:
                bsend[o, half * 4:half * 4 + 4, :] = v
    backs = offset_copies(bsend, bret, bs_sem, br_sem, -1)
    start(backs)

    diffuse(3, c_one, c_out, u_two, u_one)

    received(backs)
    for o in range(9):
        for q in range(4):
            half, at = q // 2, slice((q % 2) * 128, (q % 2) * 128 + 128)
            v = bret[o, :, at]
            swapped = pltpu.roll(v, 4, 0)
            first = rows((8, 128)) < 4
            v = jnp.where(first, v, swapped) if half == 0 else jnp.where(first, swapped, v)
            v = jnp.where(live(o, q * 128, 128), v, 0.0)
            index = cols[o, :, q * 128:q * 128 + 128]
            to = slice((o * 4 + q) * 128, (o * 4 + q) * 128 + 128)
            spread_s[:, to] = spread(split_pair(v), index >> 8, 8)
    ends = lax.dot_general(
        spread_s[...], onehot_s[...], (((1,), (1,)), ((), ())), preferred_element_type=F32)
    for h in range(8):
        aflux[:, h * 256:h * 256 + 256] = ends[h * 8:h * 8 + 4] + ends[h * 8 + 4:h * 8 + 8]

    sent(packs)
    sent(s_halos)
    sent(backs)
    for pair in u_halos:
        for copies in pair:
            sent(copies)


def per_device(atm_fields, send_cols, pair_count, remap_slot, remap_weight, land_mask, tracers, kappa):
    V, S = pltpu.VMEM, pltpu.SemaphoreType
    hbm = pl.BlockSpec(memory_space=pl.ANY)
    return pl.pallas_call(
        kernel,
        out_shape=(
            pltpu.VMEM((4, AC), F32),
            pltpu.VMEM((2, LEV, CX, CY), F32),
        ),
        in_specs=[pl.BlockSpec(memory_space=pltpu.VMEM)] + [hbm] * 7,
        out_specs=(pl.BlockSpec(memory_space=pltpu.VMEM),) * 2,
        scratch_shapes=[
            V((8, AC), F32), V((9, 1, SLOT), I32), V((K, CX, CY), I32), V((K, CX, CY), F32), V((CX, CY), I32),
            V((2, LEV, CX, CY), F32), V((LEV, CX, CY), F32),
            V((9, 8, SLOT), F32), V((9, 8, SLOT), F32), V((9, 8, 256), F32), V((9, 8, 256), F32),
            V((CX * 8, CY), F32), V((CX * 8, CY), F32), V((2, 2, CX, CY), F32),
            V((LEV * PAD, CY), F32), V((LEV, CX, CY), F32), V((CX, CY), F32),
            V((2, LEV, CX, CY), F32), V((2, LEV, CX, CY), F32),
            V((2 * LEV * PAD, CY), F32), V((2 * LEV * PAD, CY), F32), V((GROUPS, 8, 128), F32),
            V((64, 36 * 128), BF16), V((256, 36 * 128), BF16), V((2, 144, 256), BF16), V((256, 128), BF16),
            V((STEPS, 2, 2, LEV, CY), F32), V((STEPS, 2, 2, LEV, CY), F32),
            V((STEPS, 2, GROUPS, 8, 128), F32), V((STEPS, 2, 2, GROUPS, 8, 128), F32),
            V((2, LEV, CY), F32), V((2, LEV, CY), F32), V((LEV // 8, 8, 128), F32), V((2, LEV // 8, 8, 128), F32),
            S.DMA((7,)), S.DMA((9,)), S.DMA((9,)), S.DMA((9,)), S.DMA((9,)),
            S.DMA((2 * STEPS + 1, 4)), S.DMA((2 * STEPS + 1, 4)),
        ],
        compiler_params=pltpu.CompilerParams(
            collective_id=0, has_side_effects=True, vmem_limit_bytes=52 << 20),
        name="couple",
    )(pair_count, atm_fields, send_cols.transpose(1, 0, 2), remap_slot, remap_weight, land_mask, tracers, kappa)


def solution(mesh):
    return jax.shard_map(
        per_device,
        mesh=mesh,
        in_specs=(
            P(None, ("gx", "gy")),
            P(("gx", "gy"), None, None),
            P(("gx", "gy"), None),
            P(None, "gx", "gy"),
            P(None, "gx", "gy"),
            P("gx", "gy"),
            P(None, None, "gx", "gy"),
            P(None, "gx", "gy"),
        ),
        out_specs=(P(None, ("gx", "gy")), P(None, None, "gx", "gy")),
        check_vma=False,
    )
```

```python
import functools

import jax
import jax.numpy as jnp
from jax import lax
from jax.experimental import pallas as pl
from jax.experimental.pallas import tpu as pltpu
from jax.sharding import PartitionSpec as P

MESH = pl.DeviceIdType.MESH
F32, BF16, I32 = jnp.float32, jnp.bfloat16, jnp.int32
NFIELD, AC, SLOT, K, CX, CY, LEV, STEPS = 8, 2048, 512, 4, 64, 128, 32, 4
OFFSETS = [(o // 3 - 1, o % 3 - 1) for o in range(9)]
AROUND = [o for o in range(9) if o != 4]
XT = CX // 8
GROUPS = LEV // 8
GX, LOOK, SX = 16, 5, 16
PAD = CX + 16


def lanes(shape):
    return lax.broadcasted_iota(I32, shape, len(shape) - 1)


def rows(shape):
    return lax.broadcasted_iota(I32, shape, len(shape) - 2)


def split_pair(v):
    head = v.astype(BF16).astype(F32)
    return jnp.where(rows(v.shape) < 4, head, v - head)


def onehot_rows(index, count):
    at = rows((count, 128)).astype(F32).astype(BF16)
    low = jnp.broadcast_to(index.astype(F32), (16, 128)).astype(BF16)
    low = jnp.concatenate([low] * (count // 16), 0)
    return jnp.where(at == low, jnp.ones((), BF16), jnp.zeros((), BF16))


def spread(pair, high, count):
    two = jnp.concatenate([pair, pair], 0).astype(BF16)
    at = (jnp.broadcast_to(high, (16, 128)) - rows((16, 128)) // 8).astype(F32).astype(BF16)
    zero = jnp.zeros((), BF16)
    return jnp.concatenate([jnp.where(at == jnp.asarray(2 * q, BF16), two, zero) for q in range(count // 2)], 0)


def kernel(
    pc_ref, atm_hbm, cols_hbm, slot_hbm, weight_hbm, land_hbm, tr_hbm, kap_hbm,
    aflux, c_out,
    atm, cols, slot, weight, land, tr, kap,
    psend, precv, bsend, bret, remap, flux8, force,
    s_ref, a_ref, b_ref, c_one, c_two, u_one, u_two, comb,
    spread_s, onehot_s, table_s, beside_s,
    xsend, xrecv, ysend, yrecv, sxsend, sxrecv, sysend, syrecv,
    in_sem, ps_sem, pr_sem, bs_sem, br_sem, hs_sem, hr_sem,
):
    gx, gy = lax.axis_index("gx"), lax.axis_index("gy")
    n_gx, n_gy = lax.axis_size("gx"), lax.axis_size("gy")

    def inside(dx, dy):
        ok = None
        for at, d, n in ((gx, dx, n_gx), (gy, dy, n_gy)):
            c = at > 0 if d < 0 else at < n - 1 if d > 0 else None
            if c is not None:
                ok = c if ok is None else ok & c
        return ok

    sources = (atm_hbm, cols_hbm, slot_hbm, weight_hbm, land_hbm, tr_hbm, kap_hbm)
    targets = (atm, cols, slot, weight, land, tr, kap)
    loads = [pltpu.make_async_copy(a, b, in_sem.at[i]) for i, (a, b) in enumerate(zip(sources, targets))]
    for i in (0, 1, 4, 6, 5, 2, 3):
        loads[i].start()

    barrier = pltpu.get_barrier_semaphore()
    for o in AROUND:
        dx, dy = OFFSETS[o]

        @pl.when(inside(dx, dy))
        def _():
            pl.semaphore_signal(barrier, inc=1, device_id=(gx + dx, gy + dy), device_id_type=MESH)

    for side, missing in ((0, gx == 0), (1, gx == n_gx - 1)):
        @pl.when(missing)
        def _():
            for step in range(STEPS):
                for t in range(2):
                    xrecv[step, t, side] = jnp.zeros((LEV, CY), F32)
            sxrecv[side] = jnp.zeros((LEV, CY), F32)
    for side, missing in ((0, gy == 0), (1, gy == n_gy - 1)):
        @pl.when(missing)
        def _():
            for step in range(STEPS):
                for t in range(2):
                    yrecv[step, t, side] = jnp.zeros((GROUPS, 8, 128), F32)
            syrecv[side] = jnp.zeros((LEV // 8, 8, 128), F32)

    def live(o, base, width):
        count = jnp.broadcast_to(pc_ref[0:1, o:o + 1], (8, width))
        return lanes((8, width)) + base < count

    loads[0].wait()
    loads[1].wait()
    for o in range(9):
        for q in range(SLOT // 128):
            index = jnp.broadcast_to(cols[o, :, q * 128:q * 128 + 128], (8, 128))
            low, high = index & 127, index >> 7
            r = jnp.zeros((8, 128), F32)
            for h in range(AC // 128):
                got = jnp.take_along_axis(atm[:, h * 128:h * 128 + 128], low, axis=1, mode="promise_in_bounds")
                r = jnp.where(high == h, got, r)
            r = jnp.where(live(o, q * 128, 128), r, 0.0)
            if o == 4:
                precv[o, :, q * 128:q * 128 + 128] = r
            else:
                psend[o, :, q * 128:q * 128 + 128] = r

    def edge_rows(src, dst, t=0):
        for j in range(LEV // 8):
            base = (t * LEV + j * 8) * PAD + 8
            dst[0, j * 8:j * 8 + 8, :] = src[pl.ds(base + CX - 1, 8, stride=PAD), :]
            dst[1, j * 8:j * 8 + 8, :] = src[pl.ds(base, 8, stride=PAD), :]

    def halo_rows(src, dst, t=0):
        for j in range(LEV // 8):
            base = (t * LEV + j * 8) * PAD + 8
            dst[pl.ds(base - 1, 8, stride=PAD), :] = src[0, j * 8:j * 8 + 8, :]
            dst[pl.ds(base + CX, 8, stride=PAD), :] = src[1, j * 8:j * 8 + 8, :]

    def halo_copies(xs, xr, ys, yr, n):
        made = []
        for side, (dx, dy) in enumerate(((1, 0), (-1, 0), (0, 1), (0, -1))):
            src = xs.at[side] if side < 2 else ys
            dst = xr.at[side] if side < 2 else yr.at[side - 2]
            copy = pltpu.make_async_remote_copy(
                src_ref=src, dst_ref=dst, send_sem=hs_sem.at[n, side], recv_sem=hr_sem.at[n, side],
                device_id=(gx + dx, gy + dy), device_id_type=MESH)
            made.append((inside(dx, dy), inside(-dx, -dy), copy))
        return made

    def offset_copies(src, dst, ss, rs, sign):
        made = []
        for o in AROUND:
            dx, dy = OFFSETS[o][0] * sign, OFFSETS[o][1] * sign
            copy = pltpu.make_async_remote_copy(
                src_ref=src.at[o], dst_ref=dst.at[o], send_sem=ss.at[o], recv_sem=rs.at[o],
                device_id=(gx + dx, gy + dy), device_id_type=MESH)
            made.append((inside(dx, dy), inside(-dx, -dy), copy))
        return made

    def start(copies):
        for can, _, copy in copies:
            pl.when(can)(copy.start)

    def received(copies):
        for _, comes, copy in copies:
            pl.when(comes)(copy.wait_recv)

    def sent(copies):
        for can, _, copy in copies:
            pl.when(can)(copy.wait_send)

    wide = 1 + (gx > 0).astype(I32) + (gx < n_gx - 1).astype(I32)
    high = 1 + (gy > 0).astype(I32) + (gy < n_gy - 1).astype(I32)
    pl.semaphore_wait(barrier, wide * high - 1)

    packs = offset_copies(psend, precv, ps_sem, pr_sem, 1)
    start(packs)
    loads[4].wait()
    loads[6].wait()
    lane = lanes((8, 128))

    def edge(acc, v, i):
        turned = pltpu.roll(v, 2 * i + 1, 1)
        return jnp.where((lane == 2 * i) | (lane == 2 * i + 1), turned, acc)

    def start_s(g, c):
        acc = jnp.zeros((8, 128), F32)
        for dl in range(8):
            lev = g * 8 + dl
            for xt in range(XT):
                at = slice(xt * 8, xt * 8 + 8)
                wet = land[at, :].astype(F32)
                v = jnp.sqrt(kap[lev, at, :] * wet)
                s_ref[pl.ds(pl.multiple_of(lev * PAD + 8 + xt * 8, 8), 8), :] = v
                acc = edge(acc, v, dl * 8 + xt)
        sysend[g] = acc
        return c

    lax.fori_loop(0, LEV // 8, start_s, 0)
    edge_rows(s_ref, sxsend)
    s_halos = halo_copies(sxsend, sxrecv, sysend, syrecv, 2 * STEPS)
    start(s_halos)

    def edge_columns(src, t, dst, g, c):
        acc = jnp.zeros((8, 128), F32)
        for dl in range(8):
            lev = g * 8 + dl
            for xt in range(XT):
                base = (t * LEV + lev) * PAD + 8 + xt * 8
                acc = edge(acc, src[pl.ds(pl.multiple_of(base, 8), 8), :], dl * 8 + xt)
        dst[g] = acc
        return c

    def start_u(t, g, c):
        acc = jnp.zeros((8, 128), F32)
        for dl in range(8):
            lev = g * 8 + dl
            for xt in range(XT):
                s = s_ref[pl.ds(pl.multiple_of(lev * PAD + 8 + xt * 8, 8), 8), :]
                u = s * tr[t, lev, xt * 8:xt * 8 + 8, :]
                u_one[pl.ds(pl.multiple_of((t * LEV + lev) * PAD + 8 + xt * 8, 8), 8), :] = u
                acc = edge(acc, u, dl * 8 + xt)
        ysend[0, t, g] = acc
        return c

    u_halos = [
        [halo_copies(xsend.at[n, t], xrecv.at[n, t], ysend.at[n, t], yrecv.at[n, t], 2 * n + t) for t in range(2)]
        for n in range(STEPS)]
    loads[5].wait()
    for t in range(2):
        lax.fori_loop(0, GROUPS, functools.partial(start_u, t), 0)
        edge_rows(u_one, xsend.at[0, t], t)
        start(u_halos[0][t])

    def columns_in(src, groups):
        for g in range(groups):
            comb[g] = jnp.where(lane % 2 == 1, pltpu.roll(src[0, g], 1, 1), pltpu.roll(src[1, g], 127, 1))

    apart = jnp.abs(lax.broadcasted_iota(I32, (128, 128), 0) - lax.broadcasted_iota(I32, (128, 128), 1))
    near = jnp.where(apart == 1, 1.0, 0.0).astype(BF16)
    beside_s[:128] = near
    beside_s[128:] = near

    def two_parts(v):
        head = v.astype(BF16)
        return jnp.concatenate([head, (v - head.astype(F32)).astype(BF16)], 1)

    def beside(src, bases):
        blocks = [two_parts(src[pl.ds(pl.multiple_of(base, 8), CX), :]) for base in bases]
        return jnp.dot(jnp.concatenate(blocks, 0), beside_s[...], preferred_element_type=F32)

    def across(inner, packed, i):
        return inner[i * 8:i * 8 + 8] + jnp.where(at_end, pltpu.roll(packed, 127 - 2 * i, 1), 0.0)

    at_end = (lane == 0) | (lane == 127)

    def diffuse_one(step, t, c_src, c_dst, u_src, u_dst):
        received(u_halos[step][t])
        halo_rows(xrecv.at[step, t], u_src, t)
        columns_in(yrecv.at[step, t], GROUPS)
        last = step == STEPS - 1

        def group(g, c):
            packed = comb[g]
            inner = beside(u_src, [(t * LEV + g * 8 + dl) * PAD + 8 for dl in range(8)])
            added = jnp.minimum(g, 1)
            for dl in range(8):
                lev = g * 8 + dl
                above, below = jnp.maximum(lev - 1, 0), jnp.minimum(lev + 1, LEV - 1)
                for xt in range(XT):
                    at = slice(xt * 8, xt * 8 + 8)
                    s = s_ref[pl.ds(pl.multiple_of(lev * PAD + 8 + xt * 8, 8), 8), :]
                    base = (t * LEV + lev) * PAD + 8 + xt * 8
                    total = across(inner, packed, dl * 8 + xt) + u_src[pl.ds(base - 1, 8), :] + u_src[pl.ds(base + 1, 8), :]
                    new = a_ref[lev, at, :] * c_src[t, lev, at, :] + s * total
                    new = new + b_ref[at, :] * (c_src[t, above, at, :] + c_src[t, below, at, :])
                    if dl == 0:
                        new = new + force[added, t, at, :]
                    c_dst[t, lev, at, :] = new
                    if not last:
                        u_dst[pl.ds(pl.multiple_of(base, 8), 8), :] = s * new
            return c

        lax.fori_loop(0, GROUPS, group, 0)
        if not last:
            lax.fori_loop(0, GROUPS, functools.partial(edge_columns, u_dst, t, ysend.at[step + 1, t]), 0)
            edge_rows(u_dst, xsend.at[step + 1, t], t)
            start(u_halos[step + 1][t])

    def diffuse(*step):
        for t in range(2):
            diffuse_one(step[0], t, *step[1:])

    for xt in range(XT):
        at = slice(xt * 8, xt * 8 + 8)
        b_ref[at, :] = 0.05 * land[at, :].astype(F32)

    for o in range(9):
        for q in range(SLOT // 128):
            to = slice((o * 4 + q) * 128, (o * 4 + q) * 128 + 128)
            onehot_s[:, to] = onehot_rows(cols[o, :, q * 128:q * 128 + 128] & 255, 256)

    loads[2].wait()
    loads[3].wait()

    received(packs)

    table = jnp.concatenate([precv[h // 2, :, (h % 2) * 256:(h % 2) * 256 + 256] for h in range(18)], 0)
    head = table.astype(BF16)
    table_s[0] = head
    table_s[1] = (table - head.astype(F32)).astype(BF16)

    def looked_up(x):
        acc = jnp.zeros((8, 128), F32)
        for k in range(K):
            index = jnp.broadcast_to(slot[k, pl.ds(x, 1), :], (8, 128))
            low, high = index & 127, index >> 7
            r = jnp.zeros((8, 128), F32)
            for h in range(36):
                part = precv[h // 4, :, h % 4 * 128:h % 4 * 128 + 128]
                r = jnp.where(high == h, jnp.take_along_axis(part, low, axis=1, mode="promise_in_bounds"), r)
            acc = acc + jnp.broadcast_to(weight[k, pl.ds(x, 1), :], (8, 128)) * r
        remap[pl.ds(pl.multiple_of(x * 8, 8), 8), :] = acc

    def gather(i, c):
        for xx in range(GX):
            x = i * GX + xx
            if xx % (GX // LOOK) == 1:
                looked_up(x)
                continue
            hot = jnp.concatenate([onehot_rows(slot[k, pl.ds(x, 1), :] & 255, 256) for k in range(K)], 1)
            found = jnp.dot(table_s[0], hot, preferred_element_type=F32) + jnp.dot(table_s[1], hot, preferred_element_type=F32)
            acc = jnp.zeros((8, 128), F32)
            for k in range(K):
                high = jnp.broadcast_to(slot[k, pl.ds(x, 1), :], (8, 128)) >> 8
                r = jnp.zeros((8, 128), F32)
                for h in range(18):
                    r = jnp.where(high == h, found[h * 8:h * 8 + 8, k * 128:k * 128 + 128], r)
                acc = acc + jnp.broadcast_to(weight[k, pl.ds(x, 1), :], (8, 128)) * r
            remap[pl.ds(pl.multiple_of(x * 8, 8), 8), :] = acc
        return c

    lax.fori_loop(0, CX // GX, gather, 0)

    for xt in range(XT):
        at = slice(xt * 8, xt * 8 + 8)
        r = [remap[pl.ds(xt * 64 + f, 8, stride=8), :] for f in range(NFIELD)]
        wet = land[at, :].astype(F32)
        ws = jnp.sqrt(r[0] * r[0] + r[1] * r[1] + 1.0)
        heat = (ws * (r[2] - tr[0, 0, at, :]) + r[4] + r[5]) * wet
        water = (ws * (r[3] - 0.2 * tr[1, 0, at, :]) - r[6]) * wet
        sx = (ws * r[0] + 0.5 * r[7]) * wet
        sy = (ws * r[1] - 0.5 * r[7]) * wet
        for g, v in enumerate((heat, water, sx, sy)):
            flux8[pl.ds(xt * 64 + g, 8, stride=8), :] = v
            flux8[pl.ds(xt * 64 + g + 4, 8, stride=8), :] = v
        force[0, 0, at, :] = 0.05 * heat
        force[0, 1, at, :] = -0.05 * water
        force[1, 0, at, :] = jnp.zeros((8, CY), F32)
        force[1, 1, at, :] = jnp.zeros((8, CY), F32)

    received(s_halos)
    halo_rows(sxrecv, s_ref)
    columns_in(syrecv, LEV // 8)

    def centre(g, c):
        packed = comb[g]
        inner = beside(s_ref, [(g * 8 + dl) * PAD + 8 for dl in range(8)])
        for dl in range(8):
            lev = g * 8 + dl
            for xt in range(XT):
                base = lev * PAD + 8 + xt * 8
                s = s_ref[pl.ds(pl.multiple_of(base, 8), 8), :]
                total = across(inner, packed, dl * 8 + xt) + s_ref[pl.ds(base - 1, 8), :] + s_ref[pl.ds(base + 1, 8), :]
                a_ref[lev, xt * 8:xt * 8 + 8, :] = 1.0 - s * total - 2.0 * b_ref[xt * 8:xt * 8 + 8, :]
        return c

    lax.fori_loop(0, LEV // 8, centre, 0)

    diffuse(0, tr, c_one, u_one, u_two)

    def scatter_rows(i, c):
        hots, spreads = [], []
        for xx in range(SX):
            x = i * SX + xx
            for k in range(K):
                v = jnp.broadcast_to(weight[k, pl.ds(x, 1), :], (8, 128)) * flux8[pl.ds(pl.multiple_of(x * 8, 8), 8), :]
                index = slot[k, pl.ds(x, 1), :]
                hots.append(onehot_rows(index & 255, 256))
                spreads.append(spread(split_pair(v), index >> 8, 18))
        return c + lax.dot_general(
            jnp.concatenate(hots, 1), jnp.concatenate(spreads, 1), (((1,), (1,)), ((), ())), preferred_element_type=F32)

    back = lax.fori_loop(0, 2, scatter_rows, jnp.zeros((256, 144), F32))
    diffuse(1, c_one, c_two, u_two, u_one)
    back = scatter_rows(2, back)
    diffuse(2, c_two, c_one, u_one, u_two)
    back = scatter_rows(3, back).T
    for o in range(9):
        for half in range(2):
            h = o * 2 + half
            v = back[h * 8:h * 8 + 4] + back[h * 8 + 4:h * 8 + 8]
            if o == 4:
                bret[o, half * 4:half * 4 + 4, :] = v
            else:
                bsend[o, half * 4:half * 4 + 4, :] = v
    backs = offset_copies(bsend, bret, bs_sem, br_sem, -1)
    start(backs)

    diffuse(3, c_one, c_out, u_two, u_one)

    received(backs)
    for o in range(9):
        for q in range(4):
            half, at = q // 2, slice((q % 2) * 128, (q % 2) * 128 + 128)
            v = bret[o, :, at]
            swapped = pltpu.roll(v, 4, 0)
            first = rows((8, 128)) < 4
            v = jnp.where(first, v, swapped) if half == 0 else jnp.where(first, swapped, v)
            v = jnp.where(live(o, q * 128, 128), v, 0.0)
            index = cols[o, :, q * 128:q * 128 + 128]
            to = slice((o * 4 + q) * 128, (o * 4 + q) * 128 + 128)
            spread_s[:, to] = spread(split_pair(v), index >> 8, 8)
    ends = lax.dot_general(
        spread_s[...], onehot_s[...], (((1,), (1,)), ((), ())), preferred_element_type=F32)
    for h in range(8):
        aflux[:, h * 256:h * 256 + 256] = ends[h * 8:h * 8 + 4] + ends[h * 8 + 4:h * 8 + 8]

    sent(packs)
    sent(s_halos)
    sent(backs)
    for pair in u_halos:
        for copies in pair:
            sent(copies)


def per_device(atm_fields, send_cols, pair_count, remap_slot, remap_weight, land_mask, tracers, kappa):
    V, S = pltpu.VMEM, pltpu.SemaphoreType
    hbm = pl.BlockSpec(memory_space=pl.ANY)
    return pl.pallas_call(
        kernel,
        out_shape=(
            pltpu.VMEM((4, AC), F32),
            pltpu.VMEM((2, LEV, CX, CY), F32),
        ),
        in_specs=[pl.BlockSpec(memory_space=pltpu.VMEM)] + [hbm] * 7,
        out_specs=(pl.BlockSpec(memory_space=pltpu.VMEM),) * 2,
        scratch_shapes=[
            V((8, AC), F32), V((9, 1, SLOT), I32), V((K, CX, CY), I32), V((K, CX, CY), F32), V((CX, CY), I32),
            V((2, LEV, CX, CY), F32), V((LEV, CX, CY), F32),
            V((9, 8, SLOT), F32), V((9, 8, SLOT), F32), V((9, 8, 256), F32), V((9, 8, 256), F32),
            V((CX * 8, CY), F32), V((CX * 8, CY), F32), V((2, 2, CX, CY), F32),
            V((LEV * PAD, CY), F32), V((LEV, CX, CY), F32), V((CX, CY), F32),
            V((2, LEV, CX, CY), F32), V((2, LEV, CX, CY), F32),
            V((2 * LEV * PAD, CY), F32), V((2 * LEV * PAD, CY), F32), V((GROUPS, 8, 128), F32),
            V((64, 36 * 128), BF16), V((256, 36 * 128), BF16), V((2, 144, 256), BF16), V((256, 128), BF16),
            V((STEPS, 2, 2, LEV, CY), F32), V((STEPS, 2, 2, LEV, CY), F32),
            V((STEPS, 2, GROUPS, 8, 128), F32), V((STEPS, 2, 2, GROUPS, 8, 128), F32),
            V((2, LEV, CY), F32), V((2, LEV, CY), F32), V((LEV // 8, 8, 128), F32), V((2, LEV // 8, 8, 128), F32),
            S.DMA((7,)), S.DMA((9,)), S.DMA((9,)), S.DMA((9,)), S.DMA((9,)),
            S.DMA((2 * STEPS + 1, 4)), S.DMA((2 * STEPS + 1, 4)),
        ],
        compiler_params=pltpu.CompilerParams(
            collective_id=0, has_side_effects=True, vmem_limit_bytes=52 << 20),
        name="couple",
    )(pair_count, atm_fields, send_cols.transpose(1, 0, 2), remap_slot, remap_weight, land_mask, tracers, kappa)


def solution(mesh):
    return jax.shard_map(
        per_device,
        mesh=mesh,
        in_specs=(
            P(None, ("gx", "gy")),
            P(("gx", "gy"), None, None),
            P(("gx", "gy"), None),
            P(None, "gx", "gy"),
            P(None, "gx", "gy"),
            P("gx", "gy"),
            P(None, None, "gx", "gy"),
            P(None, "gx", "gy"),
        ),
        out_specs=(P(None, ("gx", "gy")), P(None, None, "gx", "gy")),
        check_vma=False,
    )
```
